256 devices in a mesh: date: 128 (over y, x, z), band: 2 (over core).
Axes of the slice: x: 4, y: 4, z: 8, core: 2. Of those that a mesh axis runs over, the one named last changes fastest.
Arguments:
- observations: float32 [8192, 8, 512], P('date', 'band'), may hold values from -6 to 6
- valid: int32 [8192, 512], P('date'), may hold values 0 or 1
- breaks: int32 [8192, 512], P('date'), may hold values 0 or 1
- refit: int32 [128, 4], P('date'), may hold values from 0 to 63, as said below
Outputs:
- coefs: float32 [128, 4, 8, 8, 512], P('date', None, 'band')
- spread: float32 [128, 4, 512], P('date')
The draws below stay inside these ranges and needn't reach their ends.
Inputs may be any that keep to these rules, and one draw needn't show every extreme that they name: `refit`: each row holds 4 different dates in increasing order.
All inputs are finite; a program needn't handle non-finite values. No bound on the sum of `valid` or of `breaks` on one device may be relied on, other than what follows from the above.
Results may differ from the reference program's by a relative error of at most 0.0003.
Values sent between devices are 32-bit elements; how exact they have to be, the bound alone decides.
A program may use at most 64 MiB of HBM per device.

```python
import math
import jax
import jax.numpy as jnp
from jax import lax

BANDS = 8
DATES_DEV = 64
PIX = 512
REFITS = 4
WINDOWS = 128
DATES = 8192


def draw_refit(key, part):
    streams = jax.random.split(jax.random.fold_in(key, 11), WINDOWS)

    def one_row(stream):
        order = jax.random.permutation(stream, DATES_DEV)
        return jnp.sort(order[:REFITS])
    return jax.vmap(one_row)(streams).astype(jnp.int32)


def touch_ends(entries, stream_key, low, largest):
    longest = entries.shape.index(max(entries.shape))
    spots = []
    for shift in (0, 1):
        where = [jax.random.randint(jax.random.fold_in(stream_key, axis), (), 0, length) for axis, length in enumerate(entries.shape)]
        where[longest] = (where[longest] + shift) % entries.shape[longest]
        spots.append(tuple(where))
    return entries.at[spots[0]].set(low).at[spots[1]].set(largest)


def block_scale(stream_key, extent, shards, smallest, largest):
    level, own = 1.0, jax.random.fold_in(stream_key, 6)
    for position, blocks in shards:
        draws = jnp.exp(jax.random.uniform(jax.random.fold_in(own, position), (blocks,), jnp.float32, smallest / len(shards), largest / len(shards)))
        level = level * jnp.repeat(draws, extent[position] // blocks).reshape([-1 if axis == position else 1 for axis in range(len(extent))])
    return level


def normal_values(rng, extent, scale, reach, cuts=(), kind=jnp.bfloat16):
    drawn = scale * jax.random.normal(rng, extent, jnp.float32)
    if cuts:
        drawn = drawn * block_scale(rng, extent, cuts, -0.22, 0.18)
    return jnp.clip(drawn, -reach, reach).astype(kind)


def setup_inputs(seed: int = 0) -> dict:
    key_of = jax.random.split(jax.random.key(seed), 5)
    observations = normal_values(key_of[0], (DATES, BANDS, PIX), 1.0, 6.0, ((0, 128), (1, 2)), jnp.float32)
    valid = touch_ends((jax.random.randint(key_of[1], (DATES, PIX), 0, 4) < 3).astype(jnp.int32), jax.random.fold_in(key_of[1], 1), 0, 1)
    breaks = touch_ends((jax.random.randint(key_of[2], (DATES, PIX), 0, 16 * DATES_DEV) < 1).astype(jnp.int32), jax.random.fold_in(key_of[2], 1), 0, 1)
    refit = draw_refit(jax.random.fold_in(key_of[4], 71), 0)
    return {"observations": observations, "valid": valid, "breaks": breaks, "refit": refit}


ridge_weight = 1.0
year_period = 365.25
upper_pairs = [(i, j) for i in range(8) for j in range(i, 8)]

def harmonics(first, length, total_dates):
    moment = (first + jnp.arange(length, dtype=jnp.int32)).astype(jnp.float32)
    scaled = 2.0 * (moment + 0.5) / total_dates - 1.0
    phase = 2.0 * math.pi * moment / year_period
    design = [jnp.ones_like(moment), scaled]
    for k in range(1, 4):
        design.append(jnp.cos(k * phase))
        design.append(jnp.sin(k * phase))
    return jnp.stack(design)

def window_weights(valid, breaks, picks):
    length = valid.shape[0]
    segment_id = jnp.cumsum(breaks, axis=0).astype(jnp.int32)
    rows_at = jnp.concatenate([picks.astype(jnp.int32), jnp.array([length - 1], jnp.int32)])
    seg_at = jnp.take(segment_id, rows_at, axis=0)
    places = jnp.arange(length, dtype=jnp.int32)
    inside = (places[None, :, None] <= rows_at[:, None, None]) & (segment_id[None] == seg_at[:, None, :])
    weight = jnp.where(inside, valid[None].astype(jnp.float32), jnp.float32(0.0))
    opened = (seg_at == 0).astype(jnp.float32)
    reset_flag = (segment_id[-1] > 0).astype(jnp.float32)
    return (weight, opened, reset_flag)

def local_sums(weight, design, table, series):
    hi = lax.Precision.HIGHEST
    gram_sum = jnp.einsum('rtp,kt->rkp', weight, table, precision=hi)
    parts = []
    for b in range(series.shape[1]):
        parts.append(jnp.einsum('rtp,it->rip', weight * series[:, b, :][None], design, precision=hi))
    moments = jnp.stack(parts, axis=1)
    sum_sq = jnp.einsum('rtp,tbp->rbp', weight, series * series, precision=hi)
    counts = lax.optimization_barrier(jnp.sum(weight, axis=1))
    return (gram_sum, moments, sum_sq, counts)

def refit_model(gram_sum, moments, sum_sq):
    entry = [[None] * 8 for _ in range(8)]
    for n, (i, j) in enumerate(upper_pairs):
        entry[i][j] = gram_sum[:, n]
        entry[j][i] = gram_sum[:, n]
    lower = [[None] * 8 for _ in range(8)]
    for j in range(8):
        diag = entry[j][j] + ridge_weight
        for k in range(j):
            diag = diag - lower[j][k] * lower[j][k]
        lower[j][j] = jnp.sqrt(diag)
        for i in range(j + 1, 8):
            value = entry[i][j]
            for k in range(j):
                value = value - lower[i][k] * lower[j][k]
            lower[i][j] = value / lower[j][j]
    rhs = [moments[:, :, i] for i in range(8)]
    forward = []
    for i in range(8):
        value = rhs[i]
        for k in range(i):
            value = value - lower[i][k][:, None] * forward[k]
        forward.append(value / lower[i][i][:, None])
    solved = [None] * 8
    for i in reversed(range(8)):
        value = forward[i]
        for k in range(i + 1, 8):
            value = value - lower[k][i][:, None] * solved[k]
        solved[i] = value / lower[i][i][:, None]
    resid = sum_sq
    for i in range(8):
        applied = entry[i][0][:, None] * solved[0]
        for j in range(1, 8):
            applied = applied + entry[i][j][:, None] * solved[j]
        resid = resid - solved[i] * (2.0 * rhs[i] - applied)
    return (jnp.stack(solved, axis=2), lax.optimization_barrier(jnp.sum(resid, axis=1)))

def reference(observations, valid, breaks, refit):
    pixels = observations.shape[2]
    nbands = observations.shape[1]

    def step(carry, window):
        start = window * DATES_DEV
        series = lax.dynamic_slice_in_dim(observations, start, DATES_DEV, 0)
        clear = lax.dynamic_slice_in_dim(valid, start, DATES_DEV, 0)
        starts = lax.dynamic_slice_in_dim(breaks, start, DATES_DEV, 0)
        picks = lax.dynamic_index_in_dim(refit, window, 0, keepdims=False)
        design = harmonics(start, DATES_DEV, DATES)
        table = jnp.stack([design[i] * design[j] for i, j in upper_pairs])
        weight, opened, reset_flag = window_weights(clear, starts, picks)
        gram_sum, moments, sum_sq, counts = local_sums(weight, design, table, series)
        c_gram, c_mom, c_sq, c_cnt = carry
        gram_at = gram_sum[:REFITS] + opened[:REFITS, None] * c_gram[None]
        mom_at = moments[:REFITS] + opened[:REFITS, None, None] * c_mom[None]
        sq_at = sum_sq[:REFITS] + opened[:REFITS, None] * c_sq[None]
        cnt_at = counts[:REFITS] + opened[:REFITS] * c_cnt[None]
        coefs, resid = refit_model(gram_at, mom_at, sq_at)
        spread = resid / jnp.maximum(cnt_at, 1.0)
        keep = reset_flag > 0.5
        new = (jnp.where(keep[None], gram_sum[REFITS], c_gram + gram_sum[REFITS]), jnp.where(keep[None, None], moments[REFITS], c_mom + moments[REFITS]), jnp.where(keep[None], sum_sq[REFITS], c_sq + sum_sq[REFITS]), jnp.where(keep, counts[REFITS], c_cnt + counts[REFITS]))
        return (new, (coefs, spread))
    init = (jnp.zeros((36, pixels), jnp.float32), jnp.zeros((nbands, 8, pixels), jnp.float32), jnp.zeros((nbands, pixels), jnp.float32), jnp.zeros((pixels,), jnp.float32))
    _, (coefs, spread) = lax.scan(step, init, jnp.arange(WINDOWS, dtype=jnp.int32))
    return (coefs, spread)
```

```python
import functools
import math

import jax
import jax.numpy as jnp
from jax import lax
from jax.experimental import pallas as pl
from jax.experimental.pallas import tpu as pltpu
from jax.sharding import Mesh
from jax.sharding import PartitionSpec as P

DATE = ("date_0", "date_1", "date_2")
MESH = pl.DeviceIdType.MESH

GROUPS = (
    ((0, 0, 0), (1, 0, 0), (2, 0, 0), (0, 1, 0), (0, 2, 0), (0, 3, 0)),
    ((0, 1, 1), (0, 2, 1), (0, 3, 1), (0, 4, 0), (0, 5, 0), (0, 6, 0)),
    ((0, 4, 1), (0, 5, 1), (0, 6, 1), (1, 1, 0), (1, 2, 0), (1, 3, 0)),
    ((1, 1, 1), (1, 2, 1), (1, 3, 1)),
)
ROW_OF = {term: 8 * g + k for g, group in enumerate(GROUPS) for k, term in enumerate(group)}
DESIGN = ((0, 0, 0), (1, 0, 0), (0, 1, 0), (0, 1, 1), (0, 2, 0), (0, 2, 1), (0, 3, 0), (0, 3, 1))
SQ_ROW, FLAG_ROW = 6, 7


def split3(value):
    high = value.astype(jnp.bfloat16)
    rest = value - high.astype(jnp.float32)
    mid = rest.astype(jnp.bfloat16)
    low = (rest - mid.astype(jnp.float32)).astype(jnp.bfloat16)
    return high, mid, low


def table(terms, rows, first, dates, total):
    row = lax.broadcasted_iota(jnp.int32, (rows, 128), 0)
    lane = lax.broadcasted_iota(jnp.int32, (rows, 128), 1)
    t = (lax.rem(lane, dates) + first).astype(jnp.float32)
    power, harmonic, shift, there = (jnp.zeros((rows, 128), jnp.float32) for _ in range(4))
    for k, term in terms.items():
        here = row == k
        power = jnp.where(here, float(term[0]), power)
        harmonic = jnp.where(here, float(term[1]), harmonic)
        shift = jnp.where(here, float(term[2]), shift)
        there = jnp.where(here, 1.0, there)
    turn = 16.0 * harmonic * t - 1461.0 * shift
    turn = turn - 5844.0 * jnp.floor(turn * (1.0 / 5844.0) + 0.5)
    wave = jnp.cos(turn * (2.0 * math.pi / 5844.0))
    s = 2.0 * (t + 0.5) / total - 1.0
    scale = jnp.where(power > 0.5, s, 1.0) * jnp.where(power > 1.5, s, 1.0)
    return wave * scale * there


def kernel(
    sizes, total,
    obs, valid, breaks, refit, coef_out, spread_out,
    ov, vv, kv, hi_v, mid_v, lo_v, zsum, ebuf, zin, before, tot, lines, back, other, resid_v,
    in_sem, a_send, a_recv, b_send, b_recv, c_send, c_recv, x_send, x_recv, r_send, r_recv,
):
    ny, nx, nz = sizes
    nl = ny * nx
    nb, dates, px = ov.shape[0] // vv.shape[0], vv.shape[0], vv.shape[1]
    tiles = px // 128
    y, x, z = (lax.axis_index(a) for a in DATE)
    c = lax.axis_index("band")
    line = y * nx + x
    window = line * nz + z

    def along(d):
        return lax.rem(z + d, nz)

    def plane(d):
        p = lax.rem(line + d, nl)
        return (p // nx, lax.rem(p, nx), z, c)

    barrier = pltpu.get_barrier_semaphore()
    for d in range(1, nz):
        for core in (c, 1 - c):
            pl.semaphore_signal(
                barrier, inc=1, device_id=(y, x, along(d), core), device_id_type=MESH
            )
    pl.semaphore_signal(barrier, inc=1, device_id=(y, x, z, 1 - c), device_id_type=MESH)
    for d in range(1, nl):
        pl.semaphore_signal(barrier, inc=1, device_id=plane(d), device_id_type=MESH)

    loads = [
        pltpu.make_async_copy(breaks, kv, in_sem.at[0]),
        pltpu.make_async_copy(valid, vv, in_sem.at[1]),
    ]
    for b in range(nb):
        loads.append(
            pltpu.make_async_copy(
                obs.at[:, b, :], ov.at[pl.ds(b * dates, dates), :], in_sem.at[2 + b]
            )
        )
    for load in loads:
        load.start()

    first = window * dates
    basis = table({v: k for k, v in ROW_OF.items()}, 32, first, dates, float(total))
    design = table(dict(enumerate(DESIGN)), 8, first, dates, float(total))
    wide = jnp.concatenate([design] * (nb * dates // 128), axis=1)
    wide = jnp.concatenate([wide] * nb, axis=0)
    row = lax.broadcasted_iota(jnp.int32, wide.shape, 0)
    col = lax.broadcasted_iota(jnp.int32, wide.shape, 1)
    wide = jnp.where(row // 8 == col // dates, wide, 0.0)
    wide = jnp.concatenate(split3(wide), axis=0)
    basis = jnp.concatenate(split3(basis[:, :dates]), axis=0)

    picks = [refit[0, r] for r in range(4)]
    reach = lax.broadcasted_iota(jnp.int32, (8 + dates, dates), 0)
    tcol = lax.broadcasted_iota(jnp.int32, (8 + dates, dates), 1)
    upto = reach
    for r in range(4):
        upto = jnp.where(reach == dates + r, picks[r], upto)
    upto = jnp.where(tcol <= upto, 1.0, 0.0).astype(jnp.bfloat16)

    loads[0].wait()
    marks = jnp.dot(
        upto, kv[...].astype(jnp.float32).astype(jnp.bfloat16), preferred_element_type=jnp.float32
    )
    seg = marks[:dates]
    seg_at = marks[dates:]
    loads[1].wait()
    clear = vv[...].astype(jnp.float32)
    for load in loads[2:]:
        load.wait()
    series = ov[...]
    high, mid, low = split3(series)
    hi_v[...] = high
    mid_v[...] = mid
    lo_v[...] = low
    square = series * series
    square = functools.reduce(
        jnp.add, [square[b * dates : (b + 1) * dates] for b in range(nb)]
    )
    trow = lax.broadcasted_iota(jnp.int32, (dates, px), 0)
    n = 8 * nb

    def sums(r):
        inside = seg == seg_at[r : r + 1]
        if r < 4:
            inside = inside & (trow <= picks[r])
        weight = jnp.where(inside, clear, 0.0)
        narrow = weight.astype(jnp.bfloat16)
        tall = jnp.concatenate([narrow] * nb, axis=0)
        one = jnp.dot(wide, tall * hi_v[...], preferred_element_type=jnp.float32)
        two = jnp.dot(wide[: 2 * n], tall * mid_v[...], preferred_element_type=jnp.float32)
        three = jnp.dot(wide[:n], tall * lo_v[...], preferred_element_type=jnp.float32)
        moment = (one[2 * n :] + two[n:] + three) + (one[n : 2 * n] + two[:n]) + one[:n]
        gram = jnp.dot(basis, narrow, preferred_element_type=jnp.float32)
        gram = (gram[64:] + gram[32:64]) + gram[:32]
        sq = jnp.sum(weight * square, axis=0, keepdims=True)
        return moment, gram, sq

    moment, gram, sq = sums(4)
    mark = jnp.where(seg_at[4:5] > 0.5, 1.0, 0.0)
    row8 = lax.broadcasted_iota(jnp.int32, (8, px), 0)
    half = n // 2
    for h in range(2):
        extra = jnp.where(c == 0, gram[8 * h : 8 * h + 8], gram[16 + 8 * h : 24 + 8 * h])
        if h == 1:
            extra = jnp.where(row8 == SQ_ROW, sq, extra)
        extra = jnp.where(row8 == FLAG_ROW, mark, extra)
        for j in range(tiles):
            lanes = slice(128 * j, 128 * j + 128)
            ebuf[h * tiles + j, :half] = moment[half * h : half * h + half, lanes]
            ebuf[h * tiles + j, half:] = extra[:, lanes]

    pl.semaphore_wait(barrier, 2 * (nz - 1) + 1 + nl - 1)
    far_first = sorted(range(1, nz), key=lambda d: -min(d, nz - d))
    a_copies = []
    for d in far_first:
        p = along(d)
        copy = pltpu.make_async_remote_copy(
            src_ref=ebuf.at[p], dst_ref=zin.at[z], send_sem=a_send.at[d], recv_sem=a_recv.at[d],
            device_id=(y, x, p, c), device_id_type=MESH,
        )
        copy.start()
        a_copies.append(copy)
    zin[z] = ebuf[z]

    row32 = lax.broadcasted_iota(jnp.int32, (32, px), 0)
    opened = []
    for r in range(4):
        moment, gram, sq = sums(r)
        gram = jnp.where(row32 == 16 * c + 8 + SQ_ROW, sq, gram)
        opened.append(jnp.where(seg_at[r : r + 1] < 0.5, 1.0, 0.0))
        for j in range(tiles):
            lanes = slice(128 * j, 128 * j + 128)
            zsum[r * tiles + j, :32] = gram[:, lanes]
            zsum[r * tiles + j, 32:] = moment[:, lanes]

    for copy in a_copies:
        copy.wait()

    flag = half + FLAG_ROW

    def join(earlier, later):
        return earlier * (1.0 - later[flag : flag + 1]) + later

    acc = zin[0]
    before[0] = jnp.zeros_like(acc)
    for k in range(1, nz):
        before[k] = acc
        acc = join(acc, zin[k])
    tot[...] = acc
    lines[line] = acc
    b_copies = []
    far_first_l = sorted(
        range(1, nl), key=lambda d: -(min(d % nx, nx - d % nx) + min(d // nx, ny - d // nx))
    )
    for d in far_first_l:
        copy = pltpu.make_async_remote_copy(
            src_ref=tot, dst_ref=lines.at[line], send_sem=b_send.at[d], recv_sem=b_recv.at[d],
            device_id=plane(d), device_id_type=MESH,
        )
        copy.start()
        b_copies.append(copy)
    for copy in b_copies:
        copy.wait()
    acc = jnp.zeros_like(acc)
    for k in range(nl):
        acc = jnp.where(k < line, join(acc, lines[k]), acc)
    for k in range(nz):
        before[k] = join(acc, before[k])
    back[z] = before[z]
    c_copies = []
    for d in far_first:
        p = along(d)
        copy = pltpu.make_async_remote_copy(
            src_ref=before.at[p], dst_ref=back.at[z], send_sem=c_send.at[d], recv_sem=c_recv.at[d],
            device_id=(y, x, p, c), device_id_type=MESH,
        )
        copy.start()
        c_copies.append(copy)
        copy = pltpu.make_async_remote_copy(
            src_ref=before.at[p, pl.ds(half, 8)], dst_ref=other.at[z],
            send_sem=x_send.at[d], recv_sem=x_recv.at[d],
            device_id=(y, x, p, 1 - c), device_id_type=MESH,
        )
        copy.start()
        c_copies.append(copy)
    copy = pltpu.make_async_remote_copy(
        src_ref=before.at[z, pl.ds(half, 8)], dst_ref=other.at[z],
        send_sem=x_send.at[0], recv_sem=x_recv.at[0],
        device_id=(y, x, z, 1 - c), device_id_type=MESH,
    )
    copy.start()
    c_copies.append(copy)
    for copy in c_copies:
        copy.wait()

    for j in range(tiles):
        mine = [back[h * tiles + j, half:] for h in range(2)]
        theirs = [other[h * tiles + j] for h in range(2)]
        pieces = [jnp.where(c == 0, mine[h], theirs[h]) for h in range(2)]
        pieces += [jnp.where(c == 0, theirs[h], mine[h]) for h in range(2)]
        pieces += [back[h * tiles + j, :half] for h in range(2)]
        carried = jnp.concatenate(pieces, axis=0)
        for r in range(4):
            lanes = slice(128 * j, 128 * j + 128)
            zsum[r * tiles + j] = zsum[r * tiles + j] + opened[r][:, lanes] * carried

    def got(power, harmonic, shift):
        return zsum[:, ROW_OF[(power, harmonic, shift)], :]

    cosine = [got(0, k, 0) for k in range(7)]
    sine = [None] + [got(0, k, 1) for k in range(1, 7)]
    entry = [[None] * 8 for _ in range(8)]
    entry[0][0] = cosine[0]
    entry[1][0] = got(1, 0, 0)
    entry[1][1] = got(2, 0, 0)
    for k in range(1, 4):
        entry[2 * k][0] = cosine[k]
        entry[2 * k + 1][0] = sine[k]
        entry[2 * k][1] = got(1, k, 0)
        entry[2 * k + 1][1] = got(1, k, 1)
        for m in range(1, k + 1):
            entry[2 * k][2 * m] = 0.5 * (cosine[k - m] + cosine[k + m])
            entry[2 * k + 1][2 * m + 1] = 0.5 * (cosine[k - m] - cosine[k + m])
            if k == m:
                entry[2 * k + 1][2 * m] = 0.5 * sine[2 * k]
            else:
                entry[2 * k + 1][2 * m] = 0.5 * (sine[k + m] + sine[k - m])
                entry[2 * k][2 * m + 1] = 0.5 * (sine[k + m] - sine[k - m])
    lower = [[None] * 8 for _ in range(8)]
    inverse = [None] * 8
    for j in range(8):
        diag = entry[j][j] + 1.0
        for k in range(j):
            diag = diag - lower[j][k] * lower[j][k]
        root = lax.rsqrt(diag)
        root = root * (1.5 - 0.5 * diag * root * root)
        inverse[j] = root
        for i in range(j + 1, 8):
            value = entry[i][j]
            for k in range(j):
                value = value - lower[i][k] * lower[j][k]
            lower[i][j] = value * root
    resid = jnp.where(c == 0, zsum[:, 8 + SQ_ROW, :], zsum[:, 24 + SQ_ROW, :])
    for b in range(nb):
        rhs = [zsum[:, 32 + 8 * b + i, :] for i in range(8)]
        forward = []
        for i in range(8):
            value = rhs[i]
            for k in range(i):
                value = value - lower[i][k] * forward[k]
            forward.append(value * inverse[i])
        solved = [None] * 8
        for i in reversed(range(8)):
            value = forward[i]
            for k in range(i + 1, 8):
                value = value - lower[k][i] * solved[k]
            solved[i] = value * inverse[i]
        for i in range(8):
            resid = resid - solved[i] * (rhs[i] + solved[i])
            for r in range(4):
                coef_out[r, b, :, i, :] = solved[i][r * tiles : (r + 1) * tiles]
    resid_v[0] = resid
    copy = pltpu.make_async_remote_copy(
        src_ref=resid_v.at[0], dst_ref=resid_v.at[1], send_sem=r_send, recv_sem=r_recv,
        device_id=(y, x, z, 1 - c), device_id_type=MESH,
    )
    copy.start()
    copy.wait()
    spread_out[...] = (resid + resid_v[1]) / jnp.maximum(cosine[0], 1.0)


def per_device(sizes, observations, valid, breaks, refit):
    dates, nb, px = observations.shape
    ny, nx, nz = sizes
    tiles = px // 128
    assert nz == 2 * tiles
    f32, bf16 = jnp.float32, jnp.bfloat16
    chunk = 4 * nb + 8
    sem = pltpu.SemaphoreType.DMA
    coefs, spread = pl.pallas_call(
        functools.partial(kernel, sizes, dates * ny * nx * nz),
        out_shape=(
            jax.ShapeDtypeStruct((4, nb, tiles, 8, 128), f32),
            jax.ShapeDtypeStruct((4 * tiles, 128), f32),
        ),
        in_specs=[pl.BlockSpec(memory_space=pl.ANY)] * 3
        + [pl.BlockSpec(memory_space=pltpu.SMEM)],
        out_specs=(pl.BlockSpec(memory_space=pltpu.VMEM), pl.BlockSpec(memory_space=pltpu.VMEM)),
        scratch_shapes=[
            pltpu.VMEM((nb * dates, px), f32),
            pltpu.VMEM((dates, px), jnp.int32),
            pltpu.VMEM((dates, px), jnp.int32),
            pltpu.VMEM((nb * dates, px), bf16),
            pltpu.VMEM((nb * dates, px), bf16),
            pltpu.VMEM((nb * dates, px), bf16),
            pltpu.VMEM((4 * tiles, 32 + 8 * nb, 128), f32),
            pltpu.VMEM((nz, chunk, 128), f32),
            pltpu.VMEM((nz, chunk, 128), f32),
            pltpu.VMEM((nz, chunk, 128), f32),
            pltpu.VMEM((chunk, 128), f32),
            pltpu.VMEM((ny * nx, chunk, 128), f32),
            pltpu.VMEM((nz, chunk, 128), f32),
            pltpu.VMEM((nz, 8, 128), f32),
            pltpu.VMEM((2, 4 * tiles, 128), f32),
            sem((2 + nb,)),
            sem((nz,)), sem((nz,)),
            sem((ny * nx,)), sem((ny * nx,)),
            sem((nz,)), sem((nz,)),
            sem((nz,)), sem((nz,)),
            sem, sem,
        ],
        compiler_params=pltpu.CompilerParams(
            collective_id=0, has_side_effects=True, vmem_limit_bytes=32 * 1024 * 1024
        ),
    )(observations, valid, breaks, refit)
    coefs = jnp.transpose(coefs, (0, 1, 3, 2, 4)).reshape(1, 4, nb, 8, px)
    return coefs, spread.reshape(1, 4, px)


def solution(mesh):
    sizes = (4, 4, 8)
    split = Mesh(mesh.devices.reshape(*sizes, mesh.shape["band"]), (*DATE, "band"))
    placed = (P(DATE, "band", None), P(DATE, None), P(DATE, None), P(DATE, None))
    return jax.shard_map(
        functools.partial(per_device, sizes),
        mesh=split,
        in_specs=placed,
        out_specs=(P(DATE, None, "band", None, None), P(DATE, None, None)),
        check_vma=False,
    )
```

```python
import functools
import math

import jax
import jax.numpy as jnp
from jax import lax
from jax.experimental import pallas as pl
from jax.experimental.pallas import tpu as pltpu
from jax.sharding import Mesh
from jax.sharding import PartitionSpec as P

DATE = ("date_0", "date_1", "date_2")
MESH = pl.DeviceIdType.MESH

GROUPS = (
    ((0, 0, 0), (1, 0, 0), (2, 0, 0), (0, 1, 0), (0, 2, 0), (0, 3, 0)),
    ((0, 1, 1), (0, 2, 1), (0, 3, 1), (0, 4, 0), (0, 5, 0), (0, 6, 0)),
    ((0, 4, 1), (0, 5, 1), (0, 6, 1), (1, 1, 0), (1, 2, 0), (1, 3, 0)),
    ((1, 1, 1), (1, 2, 1), (1, 3, 1)),
)
ROW_OF = {term: 8 * g + k for g, group in enumerate(GROUPS) for k, term in enumerate(group)}
DESIGN = ((0, 0, 0), (1, 0, 0), (0, 1, 0), (0, 1, 1), (0, 2, 0), (0, 2, 1), (0, 3, 0), (0, 3, 1))
SQ_ROW, FLAG_ROW = 6, 7


def split3(value):
    high = value.astype(jnp.bfloat16)
    rest = value - high.astype(jnp.float32)
    mid = rest.astype(jnp.bfloat16)
    low = (rest - mid.astype(jnp.float32)).astype(jnp.bfloat16)
    return high, mid, low


def table(terms, rows, first, dates, total):
    row = lax.broadcasted_iota(jnp.int32, (rows, 128), 0)
    lane = lax.broadcasted_iota(jnp.int32, (rows, 128), 1)
    t = (lax.rem(lane, dates) + first).astype(jnp.float32)
    power, harmonic, shift, there = (jnp.zeros((rows, 128), jnp.float32) for _ in range(4))
    for k, term in terms.items():
        here = row == k
        power = jnp.where(here, float(term[0]), power)
        harmonic = jnp.where(here, float(term[1]), harmonic)
        shift = jnp.where(here, float(term[2]), shift)
        there = jnp.where(here, 1.0, there)
    turn = 16.0 * harmonic * t - 1461.0 * shift
    turn = turn - 5844.0 * jnp.floor(turn * (1.0 / 5844.0) + 0.5)
    wave = jnp.cos(turn * (2.0 * math.pi / 5844.0))
    s = 2.0 * (t + 0.5) / total - 1.0
    scale = jnp.where(power > 0.5, s, 1.0) * jnp.where(power > 1.5, s, 1.0)
    return wave * scale * there


def sum_kernel(
    sizes, total,
    obs, valid, breaks, refit, at_refit,
    picked, ov, vv, kv, hi_v, mid_v, lo_v, zsum, theirs, ebuf, zin, before, tot, lines, back,
    in_sem, a_send, a_recv, b_send, b_recv, c_send, c_recv, x_send, x_recv, r_send, r_recv,
):
    ny, nx, nz = sizes
    nl = ny * nx
    nb, dates, px = ov.shape[0] // vv.shape[0], vv.shape[0], vv.shape[1]
    tiles = px // 128
    y, x, z = (lax.axis_index(a) for a in DATE)
    c = lax.axis_index("band")
    line = y * nx + x
    window = line * nz + z

    def along(d):
        return lax.rem(z + d, nz)

    def at_line(p):
        return (p // nx, lax.rem(p, nx), z, c)

    barrier = pltpu.get_barrier_semaphore()
    for d in range(1, nz):
        for core in (c, 1 - c):
            pl.semaphore_signal(
                barrier, inc=1, device_id=(y, x, along(d), core), device_id_type=MESH
            )
    pl.semaphore_signal(barrier, inc=1, device_id=(y, x, z, 1 - c), device_id_type=MESH)
    for d in range(1, nl):

        @pl.when(line >= d)
        def _():
            pl.semaphore_signal(barrier, inc=1, device_id=at_line(line - d), device_id_type=MESH)

    loads = [
        pltpu.make_async_copy(breaks, kv, in_sem.at[0]),
        pltpu.make_async_copy(valid, vv, in_sem.at[1]),
    ]
    for b in range(nb):
        loads.append(
            pltpu.make_async_copy(
                obs.at[:, b, :], ov.at[pl.ds(b * dates, dates), :], in_sem.at[2 + b]
            )
        )
    pick_load = pltpu.make_async_copy(refit, picked, in_sem.at[2 + nb])
    pick_load.start()
    for load in loads:
        load.start()

    first = window * dates
    basis = table({v: k for k, v in ROW_OF.items()}, 32, first, dates, float(total))
    design = table(dict(enumerate(DESIGN)), 8, first, dates, float(total))
    wide = jnp.concatenate([design] * (nb * dates // 128), axis=1)
    wide = jnp.concatenate([wide] * nb, axis=0)
    row = lax.broadcasted_iota(jnp.int32, wide.shape, 0)
    col = lax.broadcasted_iota(jnp.int32, wide.shape, 1)
    wide = jnp.where(row // 8 == col // dates, wide, 0.0)
    wide = jnp.concatenate(split3(wide), axis=0)
    basis = jnp.concatenate(split3(basis[:, :dates]), axis=0)

    pick_load.wait()
    picks = [picked[:, r : r + 1] for r in range(4)]
    reach = lax.broadcasted_iota(jnp.int32, (8 + dates, dates), 0)
    tcol = lax.broadcasted_iota(jnp.int32, (8 + dates, dates), 1)
    upto = reach
    for r in range(4):
        upto = jnp.where(reach == dates + r, picks[r], upto)
    upto = jnp.where(tcol <= upto, 1.0, 0.0).astype(jnp.bfloat16)

    loads[0].wait()
    marks = jnp.dot(
        upto, kv[...].astype(jnp.float32).astype(jnp.bfloat16), preferred_element_type=jnp.float32
    )
    seg = marks[:dates]
    seg_at = marks[dates:]
    loads[1].wait()
    clear = vv[...].astype(jnp.float32)
    for load in loads[2:]:
        load.wait()
    series = ov[...]
    high, mid, low = split3(series)
    hi_v[...] = high
    mid_v[...] = mid
    lo_v[...] = low
    square = series * series
    square = functools.reduce(
        jnp.add, [square[b * dates : (b + 1) * dates] for b in range(nb)]
    )
    trow = lax.broadcasted_iota(jnp.int32, (dates, px), 0)
    n = 8 * nb

    def sums(r):
        inside = seg == seg_at[r : r + 1]
        if r < 4:
            inside = inside & (trow <= picks[r])
        weight = jnp.where(inside, clear, 0.0)
        narrow = weight.astype(jnp.bfloat16)
        tall = jnp.concatenate([narrow] * nb, axis=0)
        one = jnp.dot(wide, tall * hi_v[...], preferred_element_type=jnp.float32)
        two = jnp.dot(wide[: 2 * n], tall * mid_v[...], preferred_element_type=jnp.float32)
        three = jnp.dot(wide[:n], tall * lo_v[...], preferred_element_type=jnp.float32)
        moment = (one[2 * n :] + two[n:] + three) + (one[n : 2 * n] + two[:n]) + one[:n]
        gram = jnp.dot(basis, narrow, preferred_element_type=jnp.float32)
        gram = (gram[64:] + gram[32:64]) + gram[:32]
        sq = jnp.sum(weight * square, axis=0, keepdims=True)
        return moment, gram, sq

    moment, gram, sq = sums(4)
    mark = jnp.where(seg_at[4:5] > 0.5, 1.0, 0.0)
    row8 = lax.broadcasted_iota(jnp.int32, (8, px), 0)
    half = n // 2
    for h in range(2):
        extra = jnp.where(c == 0, gram[8 * h : 8 * h + 8], gram[16 + 8 * h : 24 + 8 * h])
        if h == 1:
            extra = jnp.where(row8 == SQ_ROW, sq, extra)
        extra = jnp.where(row8 == FLAG_ROW, mark, extra)
        for j in range(tiles):
            lanes = slice(128 * j, 128 * j + 128)
            ebuf[h * tiles + j, :half] = moment[half * h : half * h + half, lanes]
            ebuf[h * tiles + j, half:] = extra[:, lanes]

    pl.semaphore_wait(barrier, 2 * (nz - 1) + 1 + nl - 1 - line)
    far_first = sorted(range(1, nz), key=lambda d: -min(d, nz - d))
    a_copies = []
    for d in far_first:
        p = along(d)
        copy = pltpu.make_async_remote_copy(
            src_ref=ebuf.at[p], dst_ref=zin.at[z], send_sem=a_send.at[d], recv_sem=a_recv.at[d],
            device_id=(y, x, p, c), device_id_type=MESH,
        )
        copy.start()
        a_copies.append(copy)
    zin[z] = ebuf[z]

    opened = []
    for r in range(4):
        moment, gram, sq = sums(r)
        square_row = jnp.where(row8 == SQ_ROW, sq, 0.0)
        opened.append(jnp.where(seg_at[r : r + 1] < 0.5, 1.0, 0.0))
        for j in range(tiles):
            lanes = slice(128 * j, 128 * j + 128)
            zsum[r * tiles + j, :n] = moment[:, lanes]
            zsum[r * tiles + j, n : n + 8] = square_row[:, lanes]
            zsum[r * tiles + j, n + 8 :] = gram[:, lanes]
    swap = pltpu.make_async_remote_copy(
        src_ref=zsum.at[:, pl.ds(0, n + 8)], dst_ref=theirs, send_sem=r_send, recv_sem=r_recv,
        device_id=(y, x, z, 1 - c), device_id_type=MESH,
    )
    swap.start()

    for copy in a_copies:
        copy.wait()

    flag = half + FLAG_ROW

    def join(earlier, later):
        return earlier * (1.0 - later[flag : flag + 1]) + later

    acc = zin[0]
    before[0] = jnp.zeros_like(acc)
    for k in range(1, nz):
        before[k] = acc
        acc = join(acc, zin[k])
    tot[...] = acc
    lines[line] = acc

    def to_line(d):
        return pltpu.make_async_remote_copy(
            src_ref=tot, dst_ref=lines.at[line], send_sem=b_send.at[d], recv_sem=b_recv.at[d],
            device_id=at_line(line + d), device_id_type=MESH,
        )

    def hops(d):
        return min(d % nx, nx - d % nx) + min(d // nx, ny - d // nx)

    for d in sorted(range(1, nl), key=lambda d: -hops(d)):

        @pl.when(line + d < nl)
        def _():
            to_line(d).start()

    for d in range(1, nl):

        @pl.when(line >= d)
        def _():
            to_line(d).wait_recv()

    acc = jnp.zeros_like(acc)
    for k in range(nl):
        acc = jnp.where(k < line, join(acc, lines[k]), acc)
    for k in range(nz):
        before[k] = join(acc, before[k])
    back[c, z] = before[z]
    c_copies = []
    for d in [*far_first, 0]:
        p = along(d)
        for core, send, recv in ((c, c_send, c_recv), (1 - c, x_send, x_recv)):
            if d == 0 and core is c:
                continue
            copy = pltpu.make_async_remote_copy(
                src_ref=before.at[p], dst_ref=back.at[c, z],
                send_sem=send.at[d], recv_sem=recv.at[d],
                device_id=(y, x, p, core), device_id_type=MESH,
            )
            copy.start()
            c_copies.append(copy)
    swap.wait()
    for copy in c_copies:
        copy.wait()

    for j in range(tiles):
        lanes = slice(128 * j, 128 * j + 128)
        by_core = [[back[core, h * tiles + j] for h in range(2)] for core in range(2)]
        pieces = []
        for me in (0, 1):
            moved = [jnp.where(c == me, by_core[0][h], by_core[1][h]) for h in range(2)]
            pieces.append(
                jnp.concatenate([moved[0][:half], moved[1][:half], moved[1][half:]], axis=0)
            )
        pieces.insert(1, jnp.concatenate([t[half:] for t in by_core[0] + by_core[1]], axis=0))
        for r in range(4):
            k = r * tiles + j
            share = opened[r][:, lanes]
            at_refit[k, : n + 8] = zsum[k, : n + 8] + share * pieces[0]
            at_refit[k, n + 8 : n + 40] = zsum[k, n + 8 :] + share * pieces[1]
            at_refit[k, n + 40 :] = theirs[k] + share * pieces[2]
    for d in range(1, nl):

        @pl.when(line + d < nl)
        def _():
            to_line(d).wait_send()


def refit_kernel(at_refit, coef_out, spread_out, coef_v, spread_v, out_sem):
    nb, tiles = coef_v.shape[1], coef_v.shape[2]
    n = 8 * nb
    rows = 8
    each = rows // tiles
    copies = []
    for part in range(4 // each):
        refit_part(at_refit, coef_v, spread_v, pl.ds(part * rows, rows), part * each, each)
        there = pl.ds(part * each, each)
        copy = pltpu.make_async_copy(coef_v.at[there], coef_out.at[there], out_sem.at[part])
        copy.start()
        copies.append(copy)
    copy = pltpu.make_async_copy(spread_v, spread_out, out_sem.at[4 // each])
    copy.start()
    for copy in [*copies, copy]:
        copy.wait()


def refit_part(at_refit, coef_v, spread_v, lines, first, each):
    nb, tiles = coef_v.shape[1], coef_v.shape[2]
    n = 8 * nb

    def got(power, harmonic, shift):
        return at_refit[lines, n + 8 + ROW_OF[(power, harmonic, shift)], :]

    cosine = [got(0, k, 0) for k in range(7)]
    sine = [None] + [got(0, k, 1) for k in range(1, 7)]
    entry = [[None] * 8 for _ in range(8)]
    entry[0][0] = cosine[0]
    entry[1][0] = got(1, 0, 0)
    entry[1][1] = got(2, 0, 0)
    for k in range(1, 4):
        entry[2 * k][0] = cosine[k]
        entry[2 * k + 1][0] = sine[k]
        entry[2 * k][1] = got(1, k, 0)
        entry[2 * k + 1][1] = got(1, k, 1)
        for m in range(1, k + 1):
            entry[2 * k][2 * m] = 0.5 * (cosine[k - m] + cosine[k + m])
            entry[2 * k + 1][2 * m + 1] = 0.5 * (cosine[k - m] - cosine[k + m])
            if k == m:
                entry[2 * k + 1][2 * m] = 0.5 * sine[2 * k]
            else:
                entry[2 * k + 1][2 * m] = 0.5 * (sine[k + m] + sine[k - m])
                entry[2 * k][2 * m + 1] = 0.5 * (sine[k + m] - sine[k - m])
    inverse = [None] * 8
    for j in range(8):
        diag = entry[j][j] + 1.0 if j == 0 else entry[j][j]
        root = lax.rsqrt(diag)
        root = root * (1.5 - 0.5 * diag * root * root)
        inverse[j] = root
        for i in range(j + 1, 8):
            entry[i][j] = entry[i][j] * root
        for i in range(j + 1, 8):
            for k in range(j + 1, i + 1):
                value = entry[i][k]
                if j == 0 and i == k:
                    value = value + 1.0
                entry[i][k] = value - entry[i][j] * entry[k][j]
    resid = []
    for mine, at in ((True, 0), (False, n + 40)):
        total = at_refit[lines, at + n + SQ_ROW, :]
        for b in range(nb):
            rhs = [at_refit[lines, at + 8 * b + i, :] for i in range(8)]
            work = list(rhs)
            for i in range(8):
                work[i] = work[i] * inverse[i]
                for k in range(i + 1, 8):
                    work[k] = work[k] - entry[k][i] * work[i]
            for i in reversed(range(8)):
                work[i] = work[i] * inverse[i]
                for k in range(i):
                    work[k] = work[k] - entry[i][k] * work[i]
            terms = [work[i] * (rhs[i] + work[i]) for i in range(8)]
            while len(terms) > 1:
                terms = [p + q for p, q in zip(terms[::2], terms[1::2])]
            total = total - terms[0]
            if mine:
                for i in range(8):
                    for r in range(each):
                        coef_v[first + r, b, :, i, :] = work[i][r * tiles : (r + 1) * tiles]
        resid.append(total)
    spread = (resid[0] + resid[1]) / jnp.maximum(cosine[0], 1.0)
    for r in range(each):
        spread_v[:, first + r, :] = spread[r * tiles : (r + 1) * tiles]


def per_device(sizes, observations, valid, breaks, refit):
    dates, nb, px = observations.shape
    ny, nx, nz = sizes
    tiles = px // 128
    assert nz == 2 * tiles
    f32, bf16 = jnp.float32, jnp.bfloat16
    chunk = 4 * nb + 8
    sem = pltpu.SemaphoreType.DMA
    args = (observations, valid, breaks, refit)
    at_refit = pl.pallas_call(
        functools.partial(sum_kernel, sizes, dates * ny * nx * nz),
        out_shape=pltpu.VMEM((4 * tiles, 48 + 16 * nb, 128), f32),
        in_specs=[pl.BlockSpec(memory_space=pltpu.HBM)] * 4,
        out_specs=pl.BlockSpec(memory_space=pltpu.VMEM),
        scratch_shapes=[
            pltpu.VMEM((1, 4), jnp.int32),
            pltpu.VMEM((nb * dates, px), f32),
            pltpu.VMEM((dates, px), jnp.int32),
            pltpu.VMEM((dates, px), jnp.int32),
            pltpu.VMEM((nb * dates, px), bf16),
            pltpu.VMEM((nb * dates, px), bf16),
            pltpu.VMEM((nb * dates, px), bf16),
            pltpu.VMEM((4 * tiles, 40 + 8 * nb, 128), f32),
            pltpu.VMEM((4 * tiles, 8 + 8 * nb, 128), f32),
            pltpu.VMEM((nz, chunk, 128), f32),
            pltpu.VMEM((nz, chunk, 128), f32),
            pltpu.VMEM((nz, chunk, 128), f32),
            pltpu.VMEM((chunk, 128), f32),
            pltpu.VMEM((ny * nx, chunk, 128), f32),
            pltpu.VMEM((2, nz, chunk, 128), f32),
            sem((3 + nb,)),
            sem((nz,)), sem((nz,)),
            sem((ny * nx,)), sem((ny * nx,)),
            sem((nz,)), sem((nz,)),
            sem((nz,)), sem((nz,)),
            sem, sem,
        ],
        compiler_params=pltpu.CompilerParams(
            collective_id=0, has_side_effects=True, vmem_limit_bytes=24 * 1024 * 1024
        ),
    )(*(pltpu.with_memory_space_constraint(a, pltpu.HBM) for a in args))
    coefs, spread = pl.pallas_call(
        refit_kernel,
        out_shape=(pltpu.HBM((4, nb, tiles, 8, 128), f32), pltpu.HBM((tiles, 4, 128), f32)),
        in_specs=[pl.BlockSpec(memory_space=pltpu.VMEM)],
        out_specs=(pl.BlockSpec(memory_space=pltpu.HBM), pl.BlockSpec(memory_space=pltpu.HBM)),
        scratch_shapes=[
            pltpu.VMEM((4, nb, tiles, 8, 128), f32),
            pltpu.VMEM((tiles, 4, 128), f32),
            sem((3,)),
        ],
        compiler_params=pltpu.CompilerParams(vmem_limit_bytes=24 * 1024 * 1024),
    )(pltpu.with_memory_space_constraint(at_refit, pltpu.VMEM))
    coefs = jnp.transpose(coefs, (0, 1, 3, 2, 4)).reshape(1, 4, nb, 8, px)
    return coefs, jnp.transpose(spread, (1, 0, 2)).reshape(1, 4, px)


def solution(mesh):
    sizes = (4, 4, 8)
    split = Mesh(mesh.devices.reshape(*sizes, mesh.shape["band"]), (*DATE, "band"))
    placed = (P(DATE, "band", None), P(DATE, None), P(DATE, None), P(DATE, None))
    return jax.shard_map(
        functools.partial(per_device, sizes),
        mesh=split,
        in_specs=placed,
        out_specs=(P(DATE, None, "band", None, None), P(DATE, None, None)),
        check_vma=False,
    )
```

```python
import functools
import math

import jax
import jax.numpy as jnp
from jax import lax
from jax.experimental import pallas as pl
from jax.experimental.pallas import tpu as pltpu
from jax.sharding import Mesh
from jax.sharding import PartitionSpec as P

DATE = ("date_0", "date_1", "date_2")
MESH = pl.DeviceIdType.MESH

GROUPS = (
    ((0, 0, 0), (1, 0, 0), (2, 0, 0), (0, 1, 0), (0, 2, 0), (0, 3, 0)),
    ((0, 1, 1), (0, 2, 1), (0, 3, 1), (0, 4, 0), (0, 5, 0), (0, 6, 0)),
    ((0, 4, 1), (0, 5, 1), (0, 6, 1), (1, 1, 0), (1, 2, 0), (1, 3, 0)),
    ((1, 1, 1), (1, 2, 1), (1, 3, 1)),
)
ROW_OF = {term: 8 * g + k for g, group in enumerate(GROUPS) for k, term in enumerate(group)}
DESIGN = ((0, 0, 0), (1, 0, 0), (0, 1, 0), (0, 1, 1), (0, 2, 0), (0, 2, 1), (0, 3, 0), (0, 3, 1))
SQ_ROW, FLAG_ROW = 6, 7


def split3(value):
    high = value.astype(jnp.bfloat16)
    rest = value - high.astype(jnp.float32)
    mid = rest.astype(jnp.bfloat16)
    low = (rest - mid.astype(jnp.float32)).astype(jnp.bfloat16)
    return high, mid, low


def table(terms, rows, first, dates, total):
    row = lax.broadcasted_iota(jnp.int32, (rows, 128), 0)
    lane = lax.broadcasted_iota(jnp.int32, (rows, 128), 1)
    t = (lax.rem(lane, dates) + first).astype(jnp.float32)
    power, harmonic, shift, there = (jnp.zeros((rows, 128), jnp.float32) for _ in range(4))
    for k, term in terms.items():
        here = row == k
        power = jnp.where(here, float(term[0]), power)
        harmonic = jnp.where(here, float(term[1]), harmonic)
        shift = jnp.where(here, float(term[2]), shift)
        there = jnp.where(here, 1.0, there)
    turn = 16.0 * harmonic * t - 1461.0 * shift
    turn = turn - 5844.0 * jnp.floor(turn * (1.0 / 5844.0) + 0.5)
    wave = jnp.cos(turn * (2.0 * math.pi / 5844.0))
    s = 2.0 * (t + 0.5) / total - 1.0
    scale = jnp.where(power > 0.5, s, 1.0) * jnp.where(power > 1.5, s, 1.0)
    return wave * scale * there


def sum_kernel(
    sizes, total,
    obs, valid, breaks, refit, at_refit,
    picked, ov, vv, kv, hi_v, mid_v, lo_v, zsum, theirs, ebuf, zin, before, tot, lines, back,
    in_sem, a_send, a_recv, b_send, b_recv, c_send, c_recv, x_send, x_recv, r_send, r_recv,
):
    ny, nx, nz = sizes
    nl = ny * nx
    nb, dates, px = ov.shape[0] // vv.shape[0], vv.shape[0], vv.shape[1]
    tiles = px // 128
    y, x, z = (lax.axis_index(a) for a in DATE)
    c = lax.axis_index("band")
    line = y * nx + x
    window = line * nz + z

    def along(d):
        return lax.rem(z + d, nz)

    def at_line(p):
        return (p // nx, lax.rem(p, nx), z, c)

    barrier = pltpu.get_barrier_semaphore()
    for d in range(1, nz):
        for core in (c, 1 - c):
            pl.semaphore_signal(
                barrier, inc=1, device_id=(y, x, along(d), core), device_id_type=MESH
            )
    pl.semaphore_signal(barrier, inc=1, device_id=(y, x, z, 1 - c), device_id_type=MESH)
    for d in range(1, nl):

        @pl.when(line >= d)
        def _():
            pl.semaphore_signal(barrier, inc=1, device_id=at_line(line - d), device_id_type=MESH)

    loads = [
        pltpu.make_async_copy(breaks, kv, in_sem.at[0]),
        pltpu.make_async_copy(valid, vv, in_sem.at[1]),
    ]
    for b in range(nb):
        loads.append(
            pltpu.make_async_copy(
                obs.at[:, b, :], ov.at[pl.ds(b * dates, dates), :], in_sem.at[2 + b]
            )
        )
    pick_load = pltpu.make_async_copy(refit, picked, in_sem.at[2 + nb])
    pick_load.start()
    for load in loads:
        load.start()

    first = window * dates
    basis = table({v: k for k, v in ROW_OF.items()}, 32, first, dates, float(total))
    design = table(dict(enumerate(DESIGN)), 8, first, dates, float(total))
    wide = jnp.concatenate([design] * (nb * dates // 128), axis=1)
    wide = jnp.concatenate([wide] * nb, axis=0)
    row = lax.broadcasted_iota(jnp.int32, wide.shape, 0)
    col = lax.broadcasted_iota(jnp.int32, wide.shape, 1)
    wide = jnp.where(row // 8 == col // dates, wide, 0.0)
    wide = jnp.concatenate(split3(wide), axis=0)
    basis = jnp.concatenate(split3(basis[:, :dates]), axis=0)

    pick_load.wait()
    picks = [picked[:, r : r + 1] for r in range(4)]
    reach = lax.broadcasted_iota(jnp.int32, (8 + dates, dates), 0)
    tcol = lax.broadcasted_iota(jnp.int32, (8 + dates, dates), 1)
    upto = reach
    for r in range(4):
        upto = jnp.where(reach == dates + r, picks[r], upto)
    upto = jnp.where(tcol <= upto, 1.0, 0.0).astype(jnp.bfloat16)

    loads[0].wait()
    marks = jnp.dot(
        upto, kv[...].astype(jnp.float32).astype(jnp.bfloat16), preferred_element_type=jnp.float32
    )
    seg = marks[:dates]
    seg_at = marks[dates:]
    loads[1].wait()
    clear = vv[...].astype(jnp.float32)
    for load in loads[2:]:
        load.wait()
    series = ov[...]
    high, mid, low = split3(series)
    hi_v[...] = high
    mid_v[...] = mid
    lo_v[...] = low
    square = series * series
    square = functools.reduce(
        jnp.add, [square[b * dates : (b + 1) * dates] for b in range(nb)]
    )
    trow = lax.broadcasted_iota(jnp.int32, (dates, px), 0)
    n = 8 * nb

    def sums(r):
        inside = seg == seg_at[r : r + 1]
        if r < 4:
            inside = inside & (trow <= picks[r])
        weight = jnp.where(inside, clear, 0.0)
        narrow = weight.astype(jnp.bfloat16)
        tall = jnp.concatenate([narrow] * nb, axis=0)
        one = jnp.dot(wide, tall * hi_v[...], preferred_element_type=jnp.float32)
        two = jnp.dot(wide[: 2 * n], tall * mid_v[...], preferred_element_type=jnp.float32)
        three = jnp.dot(wide[:n], tall * lo_v[...], preferred_element_type=jnp.float32)
        moment = (one[2 * n :] + two[n:] + three) + (one[n : 2 * n] + two[:n]) + one[:n]
        gram = jnp.dot(basis, narrow, preferred_element_type=jnp.float32)
        gram = (gram[64:] + gram[32:64]) + gram[:32]
        sq = jnp.sum(weight * square, axis=0, keepdims=True)
        return moment, gram, sq

    moment, gram, sq = sums(4)
    mark = jnp.where(seg_at[4:5] > 0.5, 1.0, 0.0)
    row8 = lax.broadcasted_iota(jnp.int32, (8, px), 0)
    half = n // 2
    for h in range(2):
        extra = jnp.where(c == 0, gram[8 * h : 8 * h + 8], gram[16 + 8 * h : 24 + 8 * h])
        if h == 1:
            extra = jnp.where(row8 == SQ_ROW, sq, extra)
        extra = jnp.where(row8 == FLAG_ROW, mark, extra)
        for j in range(tiles):
            lanes = slice(128 * j, 128 * j + 128)
            ebuf[h * tiles + j, :half] = moment[half * h : half * h + half, lanes]
            ebuf[h * tiles + j, half:] = extra[:, lanes]

    pl.semaphore_wait(barrier, 2 * (nz - 1) + 1 + nl - 1 - line)
    far_first = sorted(range(1, nz), key=lambda d: -min(d, nz - d))
    a_copies = []
    for d in far_first:
        p = along(d)
        copy = pltpu.make_async_remote_copy(
            src_ref=ebuf.at[p], dst_ref=zin.at[z], send_sem=a_send.at[d], recv_sem=a_recv.at[d],
            device_id=(y, x, p, c), device_id_type=MESH,
        )
        copy.start()
        a_copies.append(copy)
    zin[z] = ebuf[z]

    opened = []
    for r in range(4):
        moment, gram, sq = sums(r)
        square_row = jnp.where(row8 == SQ_ROW, sq, 0.0)
        opened.append(jnp.where(seg_at[r : r + 1] < 0.5, 1.0, 0.0))
        for j in range(tiles):
            lanes = slice(128 * j, 128 * j + 128)
            zsum[r * tiles + j, :n] = moment[:, lanes]
            zsum[r * tiles + j, n : n + 8] = square_row[:, lanes]
            zsum[r * tiles + j, n + 8 :] = gram[:, lanes]
    swap = pltpu.make_async_remote_copy(
        src_ref=zsum.at[:, pl.ds(0, n + 8)], dst_ref=theirs, send_sem=r_send, recv_sem=r_recv,
        device_id=(y, x, z, 1 - c), device_id_type=MESH,
    )
    swap.start()

    for copy in a_copies:
        copy.wait()

    flag = half + FLAG_ROW

    def join(earlier, later):
        return earlier * (1.0 - later[flag : flag + 1]) + later

    acc = zin[0]
    before[0] = jnp.zeros_like(acc)
    for k in range(1, nz):
        before[k] = acc
        acc = join(acc, zin[k])
    tot[...] = acc
    lines[line] = acc

    def to_line(d):
        return pltpu.make_async_remote_copy(
            src_ref=tot, dst_ref=lines.at[line], send_sem=b_send.at[d], recv_sem=b_recv.at[d],
            device_id=at_line(line + d), device_id_type=MESH,
        )

    def hops(d):
        return min(d % nx, nx - d % nx) + min(d // nx, ny - d // nx)

    for d in sorted(range(1, nl), key=lambda d: -hops(d)):

        @pl.when(line + d < nl)
        def _():
            to_line(d).start()

    for d in range(1, nl):

        @pl.when(line >= d)
        def _():
            to_line(d).wait_recv()

    acc = jnp.zeros_like(acc)
    for k in range(nl):
        acc = jnp.where(k < line, join(acc, lines[k]), acc)
    for k in range(nz):
        before[k] = join(acc, before[k])
    back[c, z] = before[z]
    c_copies = []
    for d in [*far_first, 0]:
        p = along(d)
        for core, send, recv in ((c, c_send, c_recv), (1 - c, x_send, x_recv)):
            if d == 0 and core is c:
                continue
            copy = pltpu.make_async_remote_copy(
                src_ref=before.at[p], dst_ref=back.at[c, z],
                send_sem=send.at[d], recv_sem=recv.at[d],
                device_id=(y, x, p, core), device_id_type=MESH,
            )
            copy.start()
            c_copies.append(copy)
    swap.wait()
    for copy in c_copies:
        copy.wait()

    for j in range(tiles):
        lanes = slice(128 * j, 128 * j + 128)
        by_core = [[back[core, h * tiles + j] for h in range(2)] for core in range(2)]
        pieces = []
        for me in (0, 1):
            moved = [jnp.where(c == me, by_core[0][h], by_core[1][h]) for h in range(2)]
            pieces.append(
                jnp.concatenate([moved[0][:half], moved[1][:half], moved[1][half:]], axis=0)
            )
        pieces.insert(1, jnp.concatenate([t[half:] for t in by_core[0] + by_core[1]], axis=0))
        for r in range(4):
            k = r * tiles + j
            share = opened[r][:, lanes]
            at = k * (48 + 2 * n)
            at_refit[at : at + n + 8] = zsum[k, : n + 8] + share * pieces[0]
            at_refit[at + n + 8 : at + n + 40] = zsum[k, n + 8 :] + share * pieces[1]
            at_refit[at + n + 40 : at + 2 * n + 48] = theirs[k] + share * pieces[2]
    for d in range(1, nl):

        @pl.when(line + d < nl)
        def _():
            to_line(d).wait_send()


def refit_kernel(sizes, at_refit, coef_out, spread_out, coef_v, spread_v, out_sem):
    nb, tiles = sizes
    rows = 8
    each = rows // tiles
    span = nb * tiles * 8
    copies = []
    for part in range(4 // each):
        refit_part(sizes, at_refit, coef_v, spread_v, part * rows, rows)
        there = pl.ds(part * each * span, each * span)
        copy = pltpu.make_async_copy(coef_v.at[there], coef_out.at[there], out_sem.at[part])
        copy.start()
        copies.append(copy)
    copy = pltpu.make_async_copy(spread_v, spread_out, out_sem.at[4 // each])
    copy.start()
    for copy in [*copies, copy]:
        copy.wait()


def refit_part(sizes, at_refit, coef_v, spread_v, first, rows):
    nb, tiles = sizes
    n = 8 * nb
    each = rows // tiles
    stride = 48 + 2 * n

    def load(row):
        return at_refit[pl.ds(first * stride + row, rows, stride=stride), :]

    def got(power, harmonic, shift):
        return load(n + 8 + ROW_OF[(power, harmonic, shift)])

    cosine = [got(0, k, 0) for k in range(7)]
    sine = [None] + [got(0, k, 1) for k in range(1, 7)]
    entry = [[None] * 8 for _ in range(8)]
    entry[0][0] = cosine[0]
    entry[1][0] = got(1, 0, 0)
    entry[1][1] = got(2, 0, 0)
    for k in range(1, 4):
        entry[2 * k][0] = cosine[k]
        entry[2 * k + 1][0] = sine[k]
        entry[2 * k][1] = got(1, k, 0)
        entry[2 * k + 1][1] = got(1, k, 1)
        for m in range(1, k + 1):
            entry[2 * k][2 * m] = 0.5 * (cosine[k - m] + cosine[k + m])
            entry[2 * k + 1][2 * m + 1] = 0.5 * (cosine[k - m] - cosine[k + m])
            if k == m:
                entry[2 * k + 1][2 * m] = 0.5 * sine[2 * k]
            else:
                entry[2 * k + 1][2 * m] = 0.5 * (sine[k + m] + sine[k - m])
                entry[2 * k][2 * m + 1] = 0.5 * (sine[k + m] - sine[k - m])
    inverse = [None] * 8
    for j in range(8):
        diag = entry[j][j] + 1.0 if j == 0 else entry[j][j]
        root = lax.rsqrt(diag)
        root = root * (1.5 - 0.5 * diag * root * root)
        inverse[j] = root
        for i in range(j + 1, 8):
            entry[i][j] = entry[i][j] * root
        for i in range(j + 1, 8):
            for k in range(j + 1, i + 1):
                value = entry[i][k]
                if j == 0 and i == k:
                    value = value + 1.0
                entry[i][k] = value - entry[i][j] * entry[k][j]
    resid = []
    for mine, at in ((True, 0), (False, n + 40)):
        total = load(at + n + SQ_ROW)
        for b in range(nb):
            rhs = [load(at + 8 * b + i) for i in range(8)]
            work = list(rhs)
            for i in range(8):
                work[i] = work[i] * inverse[i]
                for k in range(i + 1, 8):
                    work[k] = work[k] - entry[k][i] * work[i]
            for i in reversed(range(8)):
                work[i] = work[i] * inverse[i]
                for k in range(i):
                    work[k] = work[k] - entry[i][k] * work[i]
            terms = [work[i] * (rhs[i] + work[i]) for i in range(8)]
            while len(terms) > 1:
                terms = [p + q for p, q in zip(terms[::2], terms[1::2])]
            total = total - terms[0]
            if mine:
                for i in range(8):
                    for r in range(each):
                        at_coef = ((first // tiles + r) * nb + b) * tiles * 8 + i
                        piece = work[i][r * tiles : (r + 1) * tiles]
                        coef_v[pl.ds(at_coef, tiles, stride=8), :] = piece
        resid.append(total)
    spread = (resid[0] + resid[1]) / jnp.maximum(cosine[0], 1.0)
    for r in range(each):
        piece = spread[r * tiles : (r + 1) * tiles]
        spread_v[pl.ds(first // tiles + r, tiles, stride=4), :] = piece


def per_device(sizes, observations, valid, breaks, refit):
    dates, nb, px = observations.shape
    ny, nx, nz = sizes
    tiles = px // 128
    assert nz == 2 * tiles
    f32, bf16 = jnp.float32, jnp.bfloat16
    chunk = 4 * nb + 8
    sem = pltpu.SemaphoreType.DMA
    args = (observations, valid, breaks, refit)
    at_refit = pl.pallas_call(
        functools.partial(sum_kernel, sizes, dates * ny * nx * nz),
        out_shape=pltpu.VMEM((4 * tiles * (48 + 16 * nb), 128), f32),
        in_specs=[pl.BlockSpec(memory_space=pltpu.HBM)] * 4,
        out_specs=pl.BlockSpec(memory_space=pltpu.VMEM),
        scratch_shapes=[
            pltpu.VMEM((1, 4), jnp.int32),
            pltpu.VMEM((nb * dates, px), f32),
            pltpu.VMEM((dates, px), jnp.int32),
            pltpu.VMEM((dates, px), jnp.int32),
            pltpu.VMEM((nb * dates, px), bf16),
            pltpu.VMEM((nb * dates, px), bf16),
            pltpu.VMEM((nb * dates, px), bf16),
            pltpu.VMEM((4 * tiles, 40 + 8 * nb, 128), f32),
            pltpu.VMEM((4 * tiles, 8 + 8 * nb, 128), f32),
            pltpu.VMEM((nz, chunk, 128), f32),
            pltpu.VMEM((nz, chunk, 128), f32),
            pltpu.VMEM((nz, chunk, 128), f32),
            pltpu.VMEM((chunk, 128), f32),
            pltpu.VMEM((ny * nx, chunk, 128), f32),
            pltpu.VMEM((2, nz, chunk, 128), f32),
            sem((3 + nb,)),
            sem((nz,)), sem((nz,)),
            sem((ny * nx,)), sem((ny * nx,)),
            sem((nz,)), sem((nz,)),
            sem((nz,)), sem((nz,)),
            sem, sem,
        ],
        compiler_params=pltpu.CompilerParams(
            collective_id=0, has_side_effects=True, vmem_limit_bytes=24 * 1024 * 1024
        ),
    )(*(pltpu.with_memory_space_constraint(a, pltpu.HBM) for a in args))
    coefs, spread = pl.pallas_call(
        functools.partial(refit_kernel, (nb, tiles)),
        out_shape=(pltpu.HBM((32 * nb * tiles, 128), f32), pltpu.HBM((4 * tiles, 128), f32)),
        in_specs=[pl.BlockSpec(memory_space=pltpu.VMEM)],
        out_specs=(pl.BlockSpec(memory_space=pltpu.HBM), pl.BlockSpec(memory_space=pltpu.HBM)),
        scratch_shapes=[
            pltpu.VMEM((32 * nb * tiles, 128), f32),
            pltpu.VMEM((4 * tiles, 128), f32),
            sem((3,)),
        ],
        compiler_params=pltpu.CompilerParams(vmem_limit_bytes=24 * 1024 * 1024),
    )(pltpu.with_memory_space_constraint(at_refit, pltpu.VMEM))
    coefs = jnp.transpose(coefs.reshape(4, nb, tiles, 8, 128), (0, 1, 3, 2, 4))
    spread = jnp.transpose(spread.reshape(tiles, 4, 128), (1, 0, 2))
    return coefs.reshape(1, 4, nb, 8, px), spread.reshape(1, 4, px)


def solution(mesh):
    sizes = (4, 4, 8)
    split = Mesh(mesh.devices.reshape(*sizes, mesh.shape["band"]), (*DATE, "band"))
    placed = (P(DATE, "band", None), P(DATE, None), P(DATE, None), P(DATE, None))
    return jax.shard_map(
        functools.partial(per_device, sizes),
        mesh=split,
        in_specs=placed,
        out_specs=(P(DATE, None, "band", None, None), P(DATE, None, None)),
        check_vma=False,
    )
```

```python
import functools
import math

import jax
import jax.numpy as jnp
from jax import lax
from jax.experimental import pallas as pl
from jax.experimental.pallas import tpu as pltpu
from jax.sharding import Mesh
from jax.sharding import PartitionSpec as P

DATE = ("date_0", "date_1", "date_2")
MESH = pl.DeviceIdType.MESH

GROUPS = (
    ((0, 0, 0), (1, 0, 0), (2, 0, 0), (0, 1, 0), (0, 2, 0), (0, 3, 0)),
    ((0, 1, 1), (0, 2, 1), (0, 3, 1), (0, 4, 0), (0, 5, 0), (0, 6, 0)),
    ((0, 4, 1), (0, 5, 1), (0, 6, 1), (1, 1, 0), (1, 2, 0), (1, 3, 0)),
    ((1, 1, 1), (1, 2, 1), (1, 3, 1)),
)
ROW_OF = {term: 8 * g + k for g, group in enumerate(GROUPS) for k, term in enumerate(group)}
DESIGN = ((0, 0, 0), (1, 0, 0), (0, 1, 0), (0, 1, 1), (0, 2, 0), (0, 2, 1), (0, 3, 0), (0, 3, 1))
SQ_ROW, FLAG_ROW = 6, 7
C_ORDER = (0, 1, 2, 3, 7, 6, 5, 4)
B_ORDER = (6, 2, 10, 14, 1, 3, 5, 7, 9, 11, 13, 15, 4, 8, 12)


def split3(value):
    high = value.astype(jnp.bfloat16)
    rest = value - high.astype(jnp.float32)
    mid = rest.astype(jnp.bfloat16)
    low = (rest - mid.astype(jnp.float32)).astype(jnp.bfloat16)
    return high, mid, low


def table(terms, rows, first, dates, total):
    row = lax.broadcasted_iota(jnp.int32, (rows, 128), 0)
    lane = lax.broadcasted_iota(jnp.int32, (rows, 128), 1)
    t = (lax.rem(lane, dates) + first).astype(jnp.float32)
    power, harmonic, shift, there = (jnp.zeros((rows, 128), jnp.float32) for _ in range(4))
    for k, term in terms.items():
        here = row == k
        power = jnp.where(here, float(term[0]), power)
        harmonic = jnp.where(here, float(term[1]), harmonic)
        shift = jnp.where(here, float(term[2]), shift)
        there = jnp.where(here, 1.0, there)
    turn = 16.0 * harmonic * t - 1461.0 * shift
    turn = turn - 5844.0 * jnp.floor(turn * (1.0 / 5844.0) + 0.5)
    wave = jnp.cos(turn * (2.0 * math.pi / 5844.0))
    s = 2.0 * (t + 0.5) / total - 1.0
    scale = jnp.where(power > 0.5, s, 1.0) * jnp.where(power > 1.5, s, 1.0)
    return wave * scale * there


def sum_kernel(
    sizes, total,
    obs, valid, breaks, refit, at_refit,
    picked, ov, vv, kv, hi_v, mid_v, lo_v, zsum, theirs, ebuf, zin, before, tot, lines, back,
    in_sem, a_send, a_recv, b_send, b_recv, c_send, c_recv, x_send, x_recv, r_send, r_recv, may_send,
):
    ny, nx, nz = sizes
    nl = ny * nx
    nb, dates, px = ov.shape[0] // vv.shape[0], vv.shape[0], vv.shape[1]
    tiles = px // 128
    y, x, z = (lax.axis_index(a) for a in DATE)
    c = lax.axis_index("band")
    line = y * nx + x
    window = line * nz + z

    def along(d):
        return lax.rem(z + d, nz)

    def at_line(p):
        return (p // nx, lax.rem(p, nx), z, c)

    def rank(p):
        across, down = lax.rem(p, nx), p // nx
        across = jnp.minimum(across, nx - across)
        return (2 * across + jnp.minimum(down, ny - down)) * nl + p

    mine = rank(line)
    others = [lax.rem(line + d, nl) for d in range(1, nl)]
    lower = [(rank(p) < mine).astype(jnp.int32) for p in others]
    later = [(p > line).astype(jnp.int32) for p in others]
    greeted = sum(lower)
    answers = sum((1 - low) * late for low, late in zip(lower, later))
    far_first = sorted(range(1, nz), key=lambda d: -min(d, nz - d))

    barrier = pltpu.get_barrier_semaphore()
    for d in far_first:
        pl.semaphore_signal(barrier, inc=1, device_id=(y, x, along(d), c), device_id_type=MESH)
    pl.semaphore_signal(barrier, inc=1, device_id=(y, x, z, 1 - c), device_id_type=MESH)

    loads = [
        pltpu.make_async_copy(breaks, kv, in_sem.at[0]),
        pltpu.make_async_copy(valid, vv, in_sem.at[1]),
    ]
    for b in range(nb):
        loads.append(
            pltpu.make_async_copy(
                obs.at[:, b, :], ov.at[pl.ds(b * dates, dates), :], in_sem.at[2 + b]
            )
        )
    pick_load = pltpu.make_async_copy(refit, picked, in_sem.at[2 + nb])
    pick_load.start()
    for load in loads:
        load.start()
    for p, low in zip(others, lower):

        @pl.when(low == 0)
        def _():
            pl.semaphore_signal(barrier, inc=1, device_id=at_line(p), device_id_type=MESH)

    first = window * dates
    basis = table({v: k for k, v in ROW_OF.items()}, 32, first, dates, float(total))
    design = table(dict(enumerate(DESIGN)), 8, first, dates, float(total))
    wide = jnp.concatenate([design] * (nb * dates // 128), axis=1)
    wide = jnp.concatenate([wide] * nb, axis=0)
    row = lax.broadcasted_iota(jnp.int32, wide.shape, 0)
    col = lax.broadcasted_iota(jnp.int32, wide.shape, 1)
    wide = jnp.where(row // 8 == col // dates, wide, 0.0)
    wide = jnp.concatenate(split3(wide), axis=0)
    basis = jnp.concatenate(split3(basis[:, :dates]), axis=0)

    pick_load.wait()
    picks = [picked[:, r : r + 1] for r in range(4)]
    reach = lax.broadcasted_iota(jnp.int32, (8 + dates, dates), 0)
    tcol = lax.broadcasted_iota(jnp.int32, (8 + dates, dates), 1)
    upto = reach
    for r in range(4):
        upto = jnp.where(reach == dates + r, picks[r], upto)
    upto = jnp.where(tcol <= upto, 1.0, 0.0).astype(jnp.bfloat16)

    loads[0].wait()
    marks = jnp.dot(
        upto, kv[...].astype(jnp.float32).astype(jnp.bfloat16), preferred_element_type=jnp.float32
    )
    seg = marks[:dates]
    seg_at = marks[dates:]
    loads[1].wait()
    clear = vv[...].astype(jnp.float32)
    for load in loads[2:]:
        load.wait()
    series = ov[...]
    high, mid, low = split3(series)
    hi_v[...] = high
    mid_v[...] = mid
    lo_v[...] = low
    square = series * series
    square = functools.reduce(
        jnp.add, [square[b * dates : (b + 1) * dates] for b in range(nb)]
    )
    trow = lax.broadcasted_iota(jnp.int32, (dates, px), 0)
    n = 8 * nb

    def sums(r):
        inside = seg == seg_at[r : r + 1]
        if r < 4:
            inside = inside & (trow <= picks[r])
        weight = jnp.where(inside, clear, 0.0)
        narrow = weight.astype(jnp.bfloat16)
        tall = jnp.concatenate([narrow] * nb, axis=0)
        one = jnp.dot(wide, tall * hi_v[...], preferred_element_type=jnp.float32)
        two = jnp.dot(wide[: 2 * n], tall * mid_v[...], preferred_element_type=jnp.float32)
        three = jnp.dot(wide[:n], tall * lo_v[...], preferred_element_type=jnp.float32)
        moment = (one[2 * n :] + two[n:] + three) + (one[n : 2 * n] + two[:n]) + one[:n]
        gram = jnp.dot(basis, narrow, preferred_element_type=jnp.float32)
        gram = (gram[64:] + gram[32:64]) + gram[:32]
        sq = jnp.sum(weight * square, axis=0, keepdims=True)
        return moment, gram, sq

    moment, gram, sq = sums(4)
    mark = jnp.where(seg_at[4:5] > 0.5, 1.0, 0.0)
    row8 = lax.broadcasted_iota(jnp.int32, (8, px), 0)
    half = n // 2
    for h in range(2):
        extra = jnp.where(c == 0, gram[8 * h : 8 * h + 8], gram[16 + 8 * h : 24 + 8 * h])
        if h == 1:
            extra = jnp.where(row8 == SQ_ROW, sq, extra)
        extra = jnp.where(row8 == FLAG_ROW, mark, extra)
        for j in range(tiles):
            lanes = slice(128 * j, 128 * j + 128)
            ebuf[h * tiles + j, :half] = moment[half * h : half * h + half, lanes]
            ebuf[h * tiles + j, half:] = extra[:, lanes]

    pl.semaphore_wait(barrier, nz + greeted)
    a_copies = []
    for d in far_first:
        p = along(d)
        copy = pltpu.make_async_remote_copy(
            src_ref=ebuf.at[p], dst_ref=zin.at[z], send_sem=a_send.at[d], recv_sem=a_recv.at[d],
            device_id=(y, x, p, c), device_id_type=MESH,
        )
        copy.start()
        a_copies.append(copy)
    for p, low, late in zip(others, lower, later):

        @pl.when((low == 1) & (late == 0))
        def _():
            pl.semaphore_signal(may_send, inc=1, device_id=at_line(p), device_id_type=MESH)

    zin[z] = ebuf[z]

    opened = []
    for r in range(4):
        moment, gram, sq = sums(r)
        square_row = jnp.where(row8 == SQ_ROW, sq, 0.0)
        opened.append(jnp.where(seg_at[r : r + 1] < 0.5, 1.0, 0.0))
        for j in range(tiles):
            lanes = slice(128 * j, 128 * j + 128)
            zsum[r * tiles + j, :n] = moment[:, lanes]
            zsum[r * tiles + j, n : n + 8] = square_row[:, lanes]
            zsum[r * tiles + j, n + 8 :] = gram[:, lanes]
    swap = pltpu.make_async_remote_copy(
        src_ref=zsum.at[:, pl.ds(0, n + 8)], dst_ref=theirs, send_sem=r_send, recv_sem=r_recv,
        device_id=(y, x, z, 1 - c), device_id_type=MESH,
    )
    swap.start()

    for copy in a_copies:
        copy.wait()

    flag = half + FLAG_ROW

    def join(earlier, later):
        return earlier * (1.0 - later[flag : flag + 1]) + later

    acc = zin[0]
    before[0] = jnp.zeros_like(acc)
    for k in range(1, nz):
        before[k] = acc
        acc = join(acc, zin[k])
    tot[...] = acc
    lines[line] = acc

    def to_line(d):
        return pltpu.make_async_remote_copy(
            src_ref=tot, dst_ref=lines.at[line], send_sem=b_send.at[d], recv_sem=b_recv.at[d],
            device_id=at_line(line + d), device_id_type=MESH,
        )


    @pl.when(answers > 0)
    def _():
        pl.semaphore_wait(may_send, answers)

    for d in B_ORDER:

        @pl.when(line + d < nl)
        def _():
            to_line(d).start()

    for d in range(1, nl):

        @pl.when(line >= d)
        def _():
            to_line(d).wait_recv()

    acc = jnp.zeros_like(acc)
    for k in range(nl):
        acc = jnp.where(k < line, join(acc, lines[k]), acc)
    for k in range(nz):
        before[k] = join(acc, before[k])
    back[c, z] = before[z]

    def to_date(p, core, send, recv):
        d = lax.rem(p - z + nz, nz)
        return pltpu.make_async_remote_copy(
            src_ref=before.at[p], dst_ref=back.at[c, z], send_sem=send.at[d], recv_sem=recv.at[d],
            device_id=(y, x, p, core), device_id_type=MESH,
        )

    for p in C_ORDER:

        @pl.when(p != z)
        def _():
            to_date(p, c, c_send, c_recv).start()

        to_date(p, 1 - c, x_send, x_recv).start()

    swap.wait()
    for d in range(nz):
        if d > 0:
            to_date(along(d), c, c_send, c_recv).wait_recv()
        to_date(along(d), 1 - c, x_send, x_recv).wait_recv()

    for j in range(tiles):
        lanes = slice(128 * j, 128 * j + 128)
        by_core = [[back[core, h * tiles + j] for h in range(2)] for core in range(2)]
        pieces = []
        for me in (0, 1):
            moved = [jnp.where(c == me, by_core[0][h], by_core[1][h]) for h in range(2)]
            pieces.append(
                jnp.concatenate([moved[0][:half], moved[1][:half], moved[1][half:]], axis=0)
            )
        pieces.insert(1, jnp.concatenate([t[half:] for t in by_core[0] + by_core[1]], axis=0))
        for r in range(4):
            k = r * tiles + j
            share = opened[r][:, lanes]
            at = k * (48 + 2 * n)
            at_refit[at : at + n + 8] = zsum[k, : n + 8] + share * pieces[0]
            at_refit[at + n + 8 : at + n + 40] = zsum[k, n + 8 :] + share * pieces[1]
            at_refit[at + n + 40 : at + 2 * n + 48] = theirs[k] + share * pieces[2]
    for d in range(1, nl):

        @pl.when(line + d < nl)
        def _():
            to_line(d).wait_send()

    for d in range(1, nz):
        to_date(along(d), c, c_send, c_recv).wait_send()
    for p in range(nz):
        to_date(p, 1 - c, x_send, x_recv).wait_send()


def refit_kernel(sizes, at_refit, coef_out, spread_out, coef_v, spread_v, out_sem):
    nb, tiles = sizes
    rows = 8
    each = rows // tiles
    span = nb * tiles * 8
    copies = []
    for part in range(4 // each):
        refit_part(sizes, at_refit, coef_v, spread_v, part * rows, rows)
        there = pl.ds(part * each * span, each * span)
        copy = pltpu.make_async_copy(coef_v.at[there], coef_out.at[there], out_sem.at[part])
        copy.start()
        copies.append(copy)
    copy = pltpu.make_async_copy(spread_v, spread_out, out_sem.at[4 // each])
    copy.start()
    for copy in [*copies, copy]:
        copy.wait()


def refit_part(sizes, at_refit, coef_v, spread_v, first, rows):
    nb, tiles = sizes
    n = 8 * nb
    each = rows // tiles
    stride = 48 + 2 * n

    def load(row):
        return at_refit[pl.ds(first * stride + row, rows, stride=stride), :]

    def got(power, harmonic, shift):
        return load(n + 8 + ROW_OF[(power, harmonic, shift)])

    cosine = [got(0, k, 0) for k in range(7)]
    sine = [None] + [got(0, k, 1) for k in range(1, 7)]
    entry = [[None] * 8 for _ in range(8)]
    entry[0][0] = cosine[0]
    entry[1][0] = got(1, 0, 0)
    entry[1][1] = got(2, 0, 0)
    for k in range(1, 4):
        entry[2 * k][0] = cosine[k]
        entry[2 * k + 1][0] = sine[k]
        entry[2 * k][1] = got(1, k, 0)
        entry[2 * k + 1][1] = got(1, k, 1)
        for m in range(1, k + 1):
            entry[2 * k][2 * m] = 0.5 * (cosine[k - m] + cosine[k + m])
            entry[2 * k + 1][2 * m + 1] = 0.5 * (cosine[k - m] - cosine[k + m])
            if k == m:
                entry[2 * k + 1][2 * m] = 0.5 * sine[2 * k]
            else:
                entry[2 * k + 1][2 * m] = 0.5 * (sine[k + m] + sine[k - m])
                entry[2 * k][2 * m + 1] = 0.5 * (sine[k + m] - sine[k - m])
    inverse = [None] * 8
    for j in range(8):
        diag = entry[j][j] + 1.0 if j == 0 else entry[j][j]
        root = lax.rsqrt(diag)
        root = root * (1.5 - 0.5 * diag * root * root)
        inverse[j] = root
        for i in range(j + 1, 8):
            entry[i][j] = entry[i][j] * root
        for i in range(j + 1, 8):
            for k in range(j + 1, i + 1):
                value = entry[i][k]
                if j == 0 and i == k:
                    value = value + 1.0
                entry[i][k] = value - entry[i][j] * entry[k][j]
    resid = []
    for mine, at in ((True, 0), (False, n + 40)):
        total = load(at + n + SQ_ROW)
        for b in range(nb):
            rhs = [load(at + 8 * b + i) for i in range(8)]
            work = list(rhs)
            for i in range(8):
                work[i] = work[i] * inverse[i]
                for k in range(i + 1, 8):
                    work[k] = work[k] - entry[k][i] * work[i]
            for i in reversed(range(8)):
                work[i] = work[i] * inverse[i]
                for k in range(i):
                    work[k] = work[k] - entry[i][k] * work[i]
            terms = [work[i] * (rhs[i] + work[i]) for i in range(8)]
            while len(terms) > 1:
                terms = [p + q for p, q in zip(terms[::2], terms[1::2])]
            total = total - terms[0]
            if mine:
                for i in range(8):
                    for r in range(each):
                        at_coef = ((first // tiles + r) * nb + b) * tiles * 8 + i
                        piece = work[i][r * tiles : (r + 1) * tiles]
                        coef_v[pl.ds(at_coef, tiles, stride=8), :] = piece
        resid.append(total)
    spread = (resid[0] + resid[1]) / jnp.maximum(cosine[0], 1.0)
    for r in range(each):
        piece = spread[r * tiles : (r + 1) * tiles]
        spread_v[pl.ds(first // tiles + r, tiles, stride=4), :] = piece


def per_device(sizes, observations, valid, breaks, refit):
    dates, nb, px = observations.shape
    ny, nx, nz = sizes
    tiles = px // 128
    assert nz == 2 * tiles
    f32, bf16 = jnp.float32, jnp.bfloat16
    chunk = 4 * nb + 8
    sem = pltpu.SemaphoreType.DMA
    args = (observations, valid, breaks, refit)
    at_refit = pl.pallas_call(
        functools.partial(sum_kernel, sizes, dates * ny * nx * nz),
        out_shape=pltpu.VMEM((4 * tiles * (48 + 16 * nb), 128), f32),
        in_specs=[pl.BlockSpec(memory_space=pltpu.HBM)] * 4,
        out_specs=pl.BlockSpec(memory_space=pltpu.VMEM),
        scratch_shapes=[
            pltpu.VMEM((1, 4), jnp.int32),
            pltpu.VMEM((nb * dates, px), f32),
            pltpu.VMEM((dates, px), jnp.int32),
            pltpu.VMEM((dates, px), jnp.int32),
            pltpu.VMEM((nb * dates, px), bf16),
            pltpu.VMEM((nb * dates, px), bf16),
            pltpu.VMEM((nb * dates, px), bf16),
            pltpu.VMEM((4 * tiles, 40 + 8 * nb, 128), f32),
            pltpu.VMEM((4 * tiles, 8 + 8 * nb, 128), f32),
            pltpu.VMEM((nz, chunk, 128), f32),
            pltpu.VMEM((nz, chunk, 128), f32),
            pltpu.VMEM((nz, chunk, 128), f32),
            pltpu.VMEM((chunk, 128), f32),
            pltpu.VMEM((ny * nx, chunk, 128), f32),
            pltpu.VMEM((2, nz, chunk, 128), f32),
            sem((3 + nb,)),
            sem((nz,)), sem((nz,)),
            sem((ny * nx,)), sem((ny * nx,)),
            sem((nz,)), sem((nz,)),
            sem((nz,)), sem((nz,)),
            sem, sem,
            pltpu.SemaphoreType.REGULAR,
        ],
        compiler_params=pltpu.CompilerParams(
            collective_id=0, has_side_effects=True, vmem_limit_bytes=24 * 1024 * 1024
        ),
    )(*(pltpu.with_memory_space_constraint(a, pltpu.HBM) for a in args))
    coefs, spread = pl.pallas_call(
        functools.partial(refit_kernel, (nb, tiles)),
        out_shape=(pltpu.HBM((32 * nb * tiles, 128), f32), pltpu.HBM((4 * tiles, 128), f32)),
        in_specs=[pl.BlockSpec(memory_space=pltpu.VMEM)],
        out_specs=(pl.BlockSpec(memory_space=pltpu.HBM), pl.BlockSpec(memory_space=pltpu.HBM)),
        scratch_shapes=[
            pltpu.VMEM((32 * nb * tiles, 128), f32),
            pltpu.VMEM((4 * tiles, 128), f32),
            sem((3,)),
        ],
        compiler_params=pltpu.CompilerParams(vmem_limit_bytes=24 * 1024 * 1024),
    )(pltpu.with_memory_space_constraint(at_refit, pltpu.VMEM))
    coefs = jnp.transpose(coefs.reshape(4, nb, tiles, 8, 128), (0, 1, 3, 2, 4))
    spread = jnp.transpose(spread.reshape(tiles, 4, 128), (1, 0, 2))
    return coefs.reshape(1, 4, nb, 8, px), spread.reshape(1, 4, px)


def solution(mesh):
    sizes = (4, 4, 8)
    split = Mesh(mesh.devices.reshape(*sizes, mesh.shape["band"]), (*DATE, "band"))
    placed = (P(DATE, "band", None), P(DATE, None), P(DATE, None), P(DATE, None))
    return jax.shard_map(
        functools.partial(per_device, sizes),
        mesh=split,
        in_specs=placed,
        out_specs=(P(DATE, None, "band", None, None), P(DATE, None, None)),
        check_vma=False,
    )
```

```python
import functools
import math

import jax
import jax.numpy as jnp
from jax import lax
from jax.experimental import pallas as pl
from jax.experimental.pallas import tpu as pltpu
from jax.sharding import Mesh
from jax.sharding import PartitionSpec as P

DATE = ("date_0", "date_1", "date_2")
MESH = pl.DeviceIdType.MESH

GROUPS = (
    ((0, 0, 0), (1, 0, 0), (2, 0, 0), (0, 1, 0), (0, 2, 0), (0, 3, 0)),
    ((0, 1, 1), (0, 2, 1), (0, 3, 1), (0, 4, 0), (0, 5, 0), (0, 6, 0)),
    ((0, 4, 1), (0, 5, 1), (0, 6, 1), (1, 1, 0), (1, 2, 0), (1, 3, 0)),
    ((1, 1, 1), (1, 2, 1), (1, 3, 1)),
)
ROW_OF = {term: 8 * g + k for g, group in enumerate(GROUPS) for k, term in enumerate(group)}
DESIGN = ((0, 0, 0), (1, 0, 0), (0, 1, 0), (0, 1, 1), (0, 2, 0), (0, 2, 1), (0, 3, 0), (0, 3, 1))
SQ_ROW, FLAG_ROW = 6, 7
C_ORDER = (0, 1, 2, 3, 7, 6, 5, 4)


def split3(value):
    high = value.astype(jnp.bfloat16)
    rest = value - high.astype(jnp.float32)
    mid = rest.astype(jnp.bfloat16)
    low = (rest - mid.astype(jnp.float32)).astype(jnp.bfloat16)
    return high, mid, low


def table(terms, rows, first, dates, total):
    row = lax.broadcasted_iota(jnp.int32, (rows, 128), 0)
    lane = lax.broadcasted_iota(jnp.int32, (rows, 128), 1)
    t = (lax.rem(lane, dates) + first).astype(jnp.float32)
    power, harmonic, shift, there = (jnp.zeros((rows, 128), jnp.float32) for _ in range(4))
    for k, term in terms.items():
        here = row == k
        power = jnp.where(here, float(term[0]), power)
        harmonic = jnp.where(here, float(term[1]), harmonic)
        shift = jnp.where(here, float(term[2]), shift)
        there = jnp.where(here, 1.0, there)
    turn = 16.0 * harmonic * t - 1461.0 * shift
    turn = turn - 5844.0 * jnp.floor(turn * (1.0 / 5844.0) + 0.5)
    wave = jnp.cos(turn * (2.0 * math.pi / 5844.0))
    s = 2.0 * (t + 0.5) / total - 1.0
    scale = jnp.where(power > 0.5, s, 1.0) * jnp.where(power > 1.5, s, 1.0)
    return wave * scale * there


def sum_kernel(
    sizes, total,
    obs, valid, breaks, refit, at_refit,
    picked, ov, vv, kv, hi_v, mid_v, lo_v, zsum, theirs, ebuf, zin, before, tot, lines, back,
    in_sem, a_send, a_recv, b_send, b_recv, c_send, c_recv, x_send, x_recv, r_send, r_recv, may_send,
):
    ny, nx, nz = sizes
    nl = ny * nx
    nb, dates, px = ov.shape[0] // vv.shape[0], vv.shape[0], vv.shape[1]
    tiles = px // 128
    y, x, z = (lax.axis_index(a) for a in DATE)
    c = lax.axis_index("band")
    line = y * nx + x
    window = line * nz + z

    def along(d):
        return lax.rem(z + d, nz)

    def at_line(p):
        return (p // nx, lax.rem(p, nx), z, c)

    far_first = sorted(range(1, nz), key=lambda d: -min(d, nz - d))

    barrier = pltpu.get_barrier_semaphore()
    for d in far_first:
        pl.semaphore_signal(barrier, inc=1, device_id=(y, x, along(d), c), device_id_type=MESH)
    pl.semaphore_signal(barrier, inc=1, device_id=(y, x, z, 1 - c), device_id_type=MESH)

    loads = [
        pltpu.make_async_copy(breaks, kv, in_sem.at[0]),
        pltpu.make_async_copy(valid, vv, in_sem.at[1]),
    ]
    for b in range(nb):
        loads.append(
            pltpu.make_async_copy(
                obs.at[:, b, :], ov.at[pl.ds(b * dates, dates), :], in_sem.at[2 + b]
            )
        )
    pick_load = pltpu.make_async_copy(refit, picked, in_sem.at[2 + nb])
    pick_load.start()
    for load in loads:
        load.start()
    def rank(p):
        across, down = lax.rem(p, nx), p // nx
        across = jnp.minimum(across, nx - across)
        return (2 * across + jnp.minimum(down, ny - down)) * nl + p

    mine = rank(line)
    others = [lax.rem(line + d, nl) for d in range(1, nl)]
    lower = [(rank(p) < mine).astype(jnp.int32) for p in others]
    later = [(p > line).astype(jnp.int32) for p in others]
    greeted = sum(lower)
    answers = sum((1 - low) * late for low, late in zip(lower, later))

    for p, low in zip(others, lower):

        @pl.when(low == 0)
        def _():
            pl.semaphore_signal(barrier, inc=1, device_id=at_line(p), device_id_type=MESH)

    first = window * dates
    basis = table({v: k for k, v in ROW_OF.items()}, 32, first, dates, float(total))
    design = table(dict(enumerate(DESIGN)), 8, first, dates, float(total))
    wide = jnp.concatenate([design] * (nb * dates // 128), axis=1)
    wide = jnp.concatenate([wide] * nb, axis=0)
    row = lax.broadcasted_iota(jnp.int32, wide.shape, 0)
    col = lax.broadcasted_iota(jnp.int32, wide.shape, 1)
    wide = jnp.where(row // 8 == col // dates, wide, 0.0)
    wide = jnp.concatenate(split3(wide), axis=0)
    basis = jnp.concatenate(split3(basis[:, :dates]), axis=0)

    pick_load.wait()
    picks = [picked[:, r : r + 1] for r in range(4)]
    reach = lax.broadcasted_iota(jnp.int32, (8 + dates, dates), 0)
    tcol = lax.broadcasted_iota(jnp.int32, (8 + dates, dates), 1)
    upto = reach
    for r in range(4):
        upto = jnp.where(reach == dates + r, picks[r], upto)
    upto = jnp.where(tcol <= upto, 1.0, 0.0).astype(jnp.bfloat16)

    loads[0].wait()
    marks = jnp.dot(
        upto, kv[...].astype(jnp.float32).astype(jnp.bfloat16), preferred_element_type=jnp.float32
    )
    seg = marks[:dates]
    seg_at = marks[dates:]
    loads[1].wait()
    clear = vv[...].astype(jnp.float32)
    for load in loads[2:]:
        load.wait()
    series = ov[...]
    high, mid, low = split3(series)
    hi_v[...] = high
    mid_v[...] = mid
    lo_v[...] = low
    square = series * series
    square = functools.reduce(
        jnp.add, [square[b * dates : (b + 1) * dates] for b in range(nb)]
    )
    trow = lax.broadcasted_iota(jnp.int32, (dates, px), 0)
    n = 8 * nb

    def sums(r):
        inside = seg == seg_at[r : r + 1]
        if r < 4:
            inside = inside & (trow <= picks[r])
        weight = jnp.where(inside, clear, 0.0)
        narrow = weight.astype(jnp.bfloat16)
        tall = jnp.concatenate([narrow] * nb, axis=0)
        one = jnp.dot(wide, tall * hi_v[...], preferred_element_type=jnp.float32)
        two = jnp.dot(wide[: 2 * n], tall * mid_v[...], preferred_element_type=jnp.float32)
        three = jnp.dot(wide[:n], tall * lo_v[...], preferred_element_type=jnp.float32)
        moment = (one[2 * n :] + two[n:] + three) + (one[n : 2 * n] + two[:n]) + one[:n]
        gram = jnp.dot(basis, narrow, preferred_element_type=jnp.float32)
        gram = (gram[64:] + gram[32:64]) + gram[:32]
        sq = jnp.sum(weight * square, axis=0, keepdims=True)
        return moment, gram, sq

    moment, gram, sq = sums(4)
    mark = jnp.where(seg_at[4:5] > 0.5, 1.0, 0.0)
    row8 = lax.broadcasted_iota(jnp.int32, (8, px), 0)
    half = n // 2
    for h in range(2):
        extra = jnp.where(c == 0, gram[8 * h : 8 * h + 8], gram[16 + 8 * h : 24 + 8 * h])
        if h == 1:
            extra = jnp.where(row8 == SQ_ROW, sq, extra)
        extra = jnp.where(row8 == FLAG_ROW, mark, extra)
        for j in range(tiles):
            lanes = slice(128 * j, 128 * j + 128)
            ebuf[h * tiles + j, :half] = moment[half * h : half * h + half, lanes]
            ebuf[h * tiles + j, half:] = extra[:, lanes]

    pl.semaphore_wait(barrier, nz + greeted)

    def to_chunk(d):
        p = along(d)
        return pltpu.make_async_remote_copy(
            src_ref=ebuf.at[p], dst_ref=zin.at[z], send_sem=a_send.at[d], recv_sem=a_recv.at[d],
            device_id=(y, x, p, c), device_id_type=MESH,
        )

    for d in far_first:
        to_chunk(d).start()
    for p, low, late in zip(others, lower, later):

        @pl.when((low == 1) & (late == 0))
        def _():
            pl.semaphore_signal(may_send, inc=1, device_id=at_line(p), device_id_type=MESH)

    zin[z] = ebuf[z]

    opened = []
    for r in range(4):
        moment, gram, sq = sums(r)
        square_row = jnp.where(row8 == SQ_ROW, sq, 0.0)
        opened.append(jnp.where(seg_at[r : r + 1] < 0.5, 1.0, 0.0))
        for j in range(tiles):
            lanes = slice(128 * j, 128 * j + 128)
            zsum[r * tiles + j, :n] = moment[:, lanes]
            zsum[r * tiles + j, n : n + 8] = square_row[:, lanes]
            zsum[r * tiles + j, n + 8 :] = gram[:, lanes]
    swap = pltpu.make_async_remote_copy(
        src_ref=zsum.at[:, pl.ds(0, n + 8)], dst_ref=theirs, send_sem=r_send, recv_sem=r_recv,
        device_id=(y, x, z, 1 - c), device_id_type=MESH,
    )
    swap.start()

    flag = half + FLAG_ROW

    def join(earlier, later):
        return earlier * (1.0 - later[flag : flag + 1]) + later

    acc = jnp.zeros((half + 8, 128), jnp.float32)
    for k in range(nz):

        @pl.when(k != z)
        def _():
            to_chunk(lax.rem(z - k + nz, nz)).wait_recv()

        before[k] = acc
        acc = join(acc, zin[k])
    tot[...] = acc

    def to_line(d):
        return pltpu.make_async_remote_copy(
            src_ref=tot, dst_ref=lines.at[line], send_sem=b_send.at[d], recv_sem=b_recv.at[d],
            device_id=at_line(line + d), device_id_type=MESH,
        )


    @pl.when(answers > 0)
    def _():
        pl.semaphore_wait(may_send, answers)

    for p in sorted(range(1, nl), key=lambda p: (p % nx, -p)):

        @pl.when(p > line)
        def _():
            to_line(p - line).start()

    def fold(k, acc):
        to_line(line - k).wait_recv()
        return join(acc, lines[k])

    acc = lax.fori_loop(0, line, fold, jnp.zeros_like(acc))
    for k in range(nz):
        before[k] = join(acc, before[k])
    back[c, z] = before[z]

    def to_date(p, core, send, recv):
        d = lax.rem(p - z + nz, nz)
        return pltpu.make_async_remote_copy(
            src_ref=before.at[p], dst_ref=back.at[c, z], send_sem=send.at[d], recv_sem=recv.at[d],
            device_id=(y, x, p, core), device_id_type=MESH,
        )

    for p in C_ORDER:

        @pl.when(p != z)
        def _():
            to_date(p, c, c_send, c_recv).start()

        to_date(p, 1 - c, x_send, x_recv).start()

    swap.wait()
    for j in reversed(range(tiles)):
        lanes = slice(128 * j, 128 * j + 128)
        for q in (j, tiles + j):
            p = along(lax.rem(z - q + nz, nz))

            @pl.when(q != z)
            def _():
                to_date(p, c, c_send, c_recv).wait_recv()

            to_date(p, 1 - c, x_send, x_recv).wait_recv()

        by_core = [[back[core, h * tiles + j] for h in range(2)] for core in range(2)]
        pieces = []
        for me in (0, 1):
            moved = [jnp.where(c == me, by_core[0][h], by_core[1][h]) for h in range(2)]
            pieces.append(
                jnp.concatenate([moved[0][:half], moved[1][:half], moved[1][half:]], axis=0)
            )
        pieces.insert(1, jnp.concatenate([t[half:] for t in by_core[0] + by_core[1]], axis=0))
        for r in range(4):
            k = r * tiles + j
            share = opened[r][:, lanes]
            at = k * (48 + 2 * n)
            at_refit[at : at + n + 8] = zsum[k, : n + 8] + share * pieces[0]
            at_refit[at + n + 8 : at + n + 40] = zsum[k, n + 8 :] + share * pieces[1]
            at_refit[at + n + 40 : at + 2 * n + 48] = theirs[k] + share * pieces[2]
    for d in range(1, nl):

        @pl.when(line + d < nl)
        def _():
            to_line(d).wait_send()

    for d in range(1, nz):
        to_chunk(d).wait_send()
        to_date(along(d), c, c_send, c_recv).wait_send()
    for p in range(nz):
        to_date(p, 1 - c, x_send, x_recv).wait_send()


def refit_kernel(sizes, at_refit, coef_out, spread_out, coef_v, spread_v, out_sem):
    nb, tiles = sizes
    rows = 8
    each = rows // tiles
    span = nb * tiles * 8
    copies = []
    for part in range(4 // each):
        refit_part(sizes, at_refit, coef_v, spread_v, part * rows, rows)
        there = pl.ds(part * each * span, each * span)
        copy = pltpu.make_async_copy(coef_v.at[there], coef_out.at[there], out_sem.at[part])
        copy.start()
        copies.append(copy)
    copy = pltpu.make_async_copy(spread_v, spread_out, out_sem.at[4 // each])
    copy.start()
    for copy in [*copies, copy]:
        copy.wait()


def refit_part(sizes, at_refit, coef_v, spread_v, first, rows):
    nb, tiles = sizes
    n = 8 * nb
    each = rows // tiles
    stride = 48 + 2 * n

    def load(row):
        return at_refit[pl.ds(first * stride + row, rows, stride=stride), :]

    def got(power, harmonic, shift):
        return load(n + 8 + ROW_OF[(power, harmonic, shift)])

    cosine = [got(0, k, 0) for k in range(7)]
    sine = [None] + [got(0, k, 1) for k in range(1, 7)]
    entry = [[None] * 8 for _ in range(8)]
    entry[0][0] = cosine[0]
    entry[1][0] = got(1, 0, 0)
    entry[1][1] = got(2, 0, 0)
    for k in range(1, 4):
        entry[2 * k][0] = cosine[k]
        entry[2 * k + 1][0] = sine[k]
        entry[2 * k][1] = got(1, k, 0)
        entry[2 * k + 1][1] = got(1, k, 1)
        for m in range(1, k + 1):
            entry[2 * k][2 * m] = 0.5 * (cosine[k - m] + cosine[k + m])
            entry[2 * k + 1][2 * m + 1] = 0.5 * (cosine[k - m] - cosine[k + m])
            if k == m:
                entry[2 * k + 1][2 * m] = 0.5 * sine[2 * k]
            else:
                entry[2 * k + 1][2 * m] = 0.5 * (sine[k + m] + sine[k - m])
                entry[2 * k][2 * m + 1] = 0.5 * (sine[k + m] - sine[k - m])
    inverse = [None] * 8
    for j in range(8):
        diag = entry[j][j] + 1.0 if j == 0 else entry[j][j]
        root = lax.rsqrt(diag)
        root = root * (1.5 - 0.5 * diag * root * root)
        inverse[j] = root
        for i in range(j + 1, 8):
            entry[i][j] = entry[i][j] * root
        for i in range(j + 1, 8):
            for k in range(j + 1, i + 1):
                value = entry[i][k]
                if j == 0 and i == k:
                    value = value + 1.0
                entry[i][k] = value - entry[i][j] * entry[k][j]
    resid = []
    for mine, at in ((True, 0), (False, n + 40)):
        total = load(at + n + SQ_ROW)
        for b in range(nb):
            rhs = [load(at + 8 * b + i) for i in range(8)]
            work = list(rhs)
            for i in range(8):
                work[i] = work[i] * inverse[i]
                for k in range(i + 1, 8):
                    work[k] = work[k] - entry[k][i] * work[i]
            for i in reversed(range(8)):
                work[i] = work[i] * inverse[i]
                for k in range(i):
                    work[k] = work[k] - entry[i][k] * work[i]
            terms = [work[i] * (rhs[i] + work[i]) for i in range(8)]
            while len(terms) > 1:
                terms = [p + q for p, q in zip(terms[::2], terms[1::2])]
            total = total - terms[0]
            if mine:
                for i in range(8):
                    for r in range(each):
                        at_coef = ((first // tiles + r) * nb + b) * tiles * 8 + i
                        piece = work[i][r * tiles : (r + 1) * tiles]
                        coef_v[pl.ds(at_coef, tiles, stride=8), :] = piece
        resid.append(total)
    spread = (resid[0] + resid[1]) / jnp.maximum(cosine[0], 1.0)
    for r in range(each):
        piece = spread[r * tiles : (r + 1) * tiles]
        spread_v[pl.ds(first // tiles + r, tiles, stride=4), :] = piece


def per_device(sizes, observations, valid, breaks, refit):
    dates, nb, px = observations.shape
    ny, nx, nz = sizes
    tiles = px // 128
    assert nz == 2 * tiles
    f32, bf16 = jnp.float32, jnp.bfloat16
    chunk = 4 * nb + 8
    sem = pltpu.SemaphoreType.DMA
    args = (observations, valid, breaks, refit)
    at_refit = pl.pallas_call(
        functools.partial(sum_kernel, sizes, dates * ny * nx * nz),
        out_shape=pltpu.VMEM((4 * tiles * (48 + 16 * nb), 128), f32),
        in_specs=[pl.BlockSpec(memory_space=pltpu.HBM)] * 4,
        out_specs=pl.BlockSpec(memory_space=pltpu.VMEM),
        scratch_shapes=[
            pltpu.VMEM((1, 4), jnp.int32),
            pltpu.VMEM((nb * dates, px), f32),
            pltpu.VMEM((dates, px), jnp.int32),
            pltpu.VMEM((dates, px), jnp.int32),
            pltpu.VMEM((nb * dates, px), bf16),
            pltpu.VMEM((nb * dates, px), bf16),
            pltpu.VMEM((nb * dates, px), bf16),
            pltpu.VMEM((4 * tiles, 40 + 8 * nb, 128), f32),
            pltpu.VMEM((4 * tiles, 8 + 8 * nb, 128), f32),
            pltpu.VMEM((nz, chunk, 128), f32),
            pltpu.VMEM((nz, chunk, 128), f32),
            pltpu.VMEM((nz, chunk, 128), f32),
            pltpu.VMEM((chunk, 128), f32),
            pltpu.VMEM((ny * nx, chunk, 128), f32),
            pltpu.VMEM((2, nz, chunk, 128), f32),
            sem((3 + nb,)),
            sem((nz,)), sem((nz,)),
            sem((ny * nx,)), sem((ny * nx,)),
            sem((nz,)), sem((nz,)),
            sem((nz,)), sem((nz,)),
            sem, sem,
            pltpu.SemaphoreType.REGULAR,
        ],
        compiler_params=pltpu.CompilerParams(
            collective_id=0, has_side_effects=True, vmem_limit_bytes=24 * 1024 * 1024
        ),
    )(*(pltpu.with_memory_space_constraint(a, pltpu.HBM) for a in args))
    coefs, spread = pl.pallas_call(
        functools.partial(refit_kernel, (nb, tiles)),
        out_shape=(pltpu.HBM((32 * nb * tiles, 128), f32), pltpu.HBM((4 * tiles, 128), f32)),
        in_specs=[pl.BlockSpec(memory_space=pltpu.VMEM)],
        out_specs=(pl.BlockSpec(memory_space=pltpu.HBM), pl.BlockSpec(memory_space=pltpu.HBM)),
        scratch_shapes=[
            pltpu.VMEM((32 * nb * tiles, 128), f32),
            pltpu.VMEM((4 * tiles, 128), f32),
            sem((3,)),
        ],
        compiler_params=pltpu.CompilerParams(vmem_limit_bytes=24 * 1024 * 1024),
    )(pltpu.with_memory_space_constraint(at_refit, pltpu.VMEM))
    coefs = jnp.transpose(coefs.reshape(4, nb, tiles, 8, 128), (0, 1, 3, 2, 4))
    spread = jnp.transpose(spread.reshape(tiles, 4, 128), (1, 0, 2))
    return coefs.reshape(1, 4, nb, 8, px), spread.reshape(1, 4, px)


def solution(mesh):
    sizes = (4, 4, 8)
    split = Mesh(mesh.devices.reshape(*sizes, mesh.shape["band"]), (*DATE, "band"))
    placed = (P(DATE, "band", None), P(DATE, None), P(DATE, None), P(DATE, None))
    return jax.shard_map(
        functools.partial(per_device, sizes),
        mesh=split,
        in_specs=placed,
        out_specs=(P(DATE, None, "band", None, None), P(DATE, None, None)),
        check_vma=False,
    )
```

```python
import functools
import math

import jax
import jax.numpy as jnp
from jax import lax
from jax.experimental import pallas as pl
from jax.experimental.pallas import tpu as pltpu
from jax.sharding import Mesh
from jax.sharding import PartitionSpec as P

DATE = ("date_0", "date_1", "date_2")
MESH = pl.DeviceIdType.MESH

GROUPS = (
    ((0, 0, 0), (1, 0, 0), (2, 0, 0), (0, 1, 0), (0, 2, 0), (0, 3, 0)),
    ((0, 1, 1), (0, 2, 1), (0, 3, 1), (0, 4, 0), (0, 5, 0), (0, 6, 0)),
    ((0, 4, 1), (0, 5, 1), (0, 6, 1), (1, 1, 0), (1, 2, 0), (1, 3, 0)),
    ((1, 1, 1), (1, 2, 1), (1, 3, 1)),
)
ROW_OF = {term: 8 * g + k for g, group in enumerate(GROUPS) for k, term in enumerate(group)}
DESIGN = ((0, 0, 0), (1, 0, 0), (0, 1, 0), (0, 1, 1), (0, 2, 0), (0, 2, 1), (0, 3, 0), (0, 3, 1))
SQ_ROW, FLAG_ROW = 6, 7
C_ORDER = (0, 1, 2, 3, 7, 6, 5, 4)


def split3(value):
    high = value.astype(jnp.bfloat16)
    rest = value - high.astype(jnp.float32)
    mid = rest.astype(jnp.bfloat16)
    low = (rest - mid.astype(jnp.float32)).astype(jnp.bfloat16)
    return high, mid, low


def table(terms, rows, first, dates, total):
    row = lax.broadcasted_iota(jnp.int32, (rows, 128), 0)
    lane = lax.broadcasted_iota(jnp.int32, (rows, 128), 1)
    t = (lax.rem(lane, dates) + first).astype(jnp.float32)
    power, harmonic, shift, there = (jnp.zeros((rows, 128), jnp.float32) for _ in range(4))
    for k, term in terms.items():
        here = row == k
        power = jnp.where(here, float(term[0]), power)
        harmonic = jnp.where(here, float(term[1]), harmonic)
        shift = jnp.where(here, float(term[2]), shift)
        there = jnp.where(here, 1.0, there)
    turn = 16.0 * harmonic * t - 1461.0 * shift
    turn = turn - 5844.0 * jnp.floor(turn * (1.0 / 5844.0) + 0.5)
    wave = jnp.cos(turn * (2.0 * math.pi / 5844.0))
    s = 2.0 * (t + 0.5) / total - 1.0
    scale = jnp.where(power > 0.5, s, 1.0) * jnp.where(power > 1.5, s, 1.0)
    return wave * scale * there


def sum_kernel(
    sizes, total,
    obs, valid, breaks, refit, at_refit,
    picked, ov, vv, kv, hi_v, mid_v, lo_v, zsum, theirs, ebuf, zin, before, tot, lines, back,
    in_sem, a_send, a_recv, b_send, b_recv, c_send, c_recv, x_send, x_recv, r_send, r_recv, may_send,
):
    ny, nx, nz = sizes
    nl = ny * nx
    nb, dates, px = ov.shape[0] // vv.shape[0], vv.shape[0], vv.shape[1]
    tiles = px // 128
    y, x, z = (lax.axis_index(a) for a in DATE)
    c = lax.axis_index("band")
    line = y * nx + x
    window = line * nz + z

    def along(d):
        return lax.rem(z + d, nz)

    def at_line(p):
        return (p // nx, lax.rem(p, nx), z, c)

    far_first = sorted(range(1, nz), key=lambda d: -min(d, nz - d))

    barrier = pltpu.get_barrier_semaphore()
    for d in far_first:
        pl.semaphore_signal(barrier, inc=1, device_id=(y, x, along(d), c), device_id_type=MESH)
    pl.semaphore_signal(barrier, inc=1, device_id=(y, x, z, 1 - c), device_id_type=MESH)

    loads = [
        pltpu.make_async_copy(breaks, kv, in_sem.at[0]),
        pltpu.make_async_copy(valid, vv, in_sem.at[1]),
    ]
    for b in range(nb):
        loads.append(
            pltpu.make_async_copy(
                obs.at[:, b, :], ov.at[pl.ds(b * dates, dates), :], in_sem.at[2 + b]
            )
        )
    pick_load = pltpu.make_async_copy(refit, picked, in_sem.at[2 + nb])
    pick_load.start()
    for load in loads:
        load.start()
    def rank(p):
        across, down = lax.rem(p, nx), p // nx
        across = jnp.minimum(across, nx - across)
        return (2 * across + jnp.minimum(down, ny - down)) * nl + p

    mine = rank(line)
    others = [lax.rem(line + d, nl) for d in range(1, nl)]
    lower = [(rank(p) < mine).astype(jnp.int32) for p in others]
    later = [(p > line).astype(jnp.int32) for p in others]
    greeted = sum(lower)
    answers = sum((1 - low) * late for low, late in zip(lower, later))

    for p, low in zip(others, lower):

        @pl.when(low == 0)
        def _():
            pl.semaphore_signal(barrier, inc=1, device_id=at_line(p), device_id_type=MESH)

    first = window * dates
    basis = table({v: k for k, v in ROW_OF.items()}, 32, first, dates, float(total))
    design = table(dict(enumerate(DESIGN)), 8, first, dates, float(total))
    wide = jnp.concatenate([design] * (nb * dates // 128), axis=1)
    wide = jnp.concatenate([wide] * nb, axis=0)
    row = lax.broadcasted_iota(jnp.int32, wide.shape, 0)
    col = lax.broadcasted_iota(jnp.int32, wide.shape, 1)
    wide = jnp.where(row // 8 == col // dates, wide, 0.0)
    wide = jnp.concatenate(split3(wide), axis=0)
    basis = jnp.concatenate(split3(basis[:, :dates]), axis=0)

    pick_load.wait()
    picks = [picked[:, r : r + 1] for r in range(4)]
    reach = lax.broadcasted_iota(jnp.int32, (8 + dates, dates), 0)
    tcol = lax.broadcasted_iota(jnp.int32, (8 + dates, dates), 1)
    upto = reach
    for r in range(4):
        upto = jnp.where(reach == dates + r, picks[r], upto)
    upto = jnp.where(tcol <= upto, 1.0, 0.0).astype(jnp.bfloat16)

    loads[0].wait()
    marks = jnp.dot(
        upto, kv[...].astype(jnp.float32).astype(jnp.bfloat16), preferred_element_type=jnp.float32
    )
    seg = marks[:dates]
    seg_at = marks[dates:]
    loads[1].wait()
    clear = vv[...].astype(jnp.float32)
    for load in loads[2:]:
        load.wait()
    series = ov[...]
    high, mid, low = split3(series)
    hi_v[...] = high
    mid_v[...] = mid
    lo_v[...] = low
    square = series * series
    square = functools.reduce(
        jnp.add, [square[b * dates : (b + 1) * dates] for b in range(nb)]
    )
    trow = lax.broadcasted_iota(jnp.int32, (dates, px), 0)
    n = 8 * nb

    def sums(r):
        inside = seg == seg_at[r : r + 1]
        if r < 4:
            inside = inside & (trow <= picks[r])
        weight = jnp.where(inside, clear, 0.0)
        narrow = weight.astype(jnp.bfloat16)
        tall = jnp.concatenate([narrow] * nb, axis=0)
        one = jnp.dot(wide, tall * hi_v[...], preferred_element_type=jnp.float32)
        two = jnp.dot(wide[: 2 * n], tall * mid_v[...], preferred_element_type=jnp.float32)
        three = jnp.dot(wide[:n], tall * lo_v[...], preferred_element_type=jnp.float32)
        moment = (one[2 * n :] + two[n:] + three) + (one[n : 2 * n] + two[:n]) + one[:n]
        gram = jnp.dot(basis, narrow, preferred_element_type=jnp.float32)
        gram = (gram[64:] + gram[32:64]) + gram[:32]
        sq = jnp.sum(weight * square, axis=0, keepdims=True)
        return moment, gram, sq

    moment, gram, sq = sums(4)
    mark = jnp.where(seg_at[4:5] > 0.5, 1.0, 0.0)
    row8 = lax.broadcasted_iota(jnp.int32, (8, px), 0)
    half = n // 2
    for h in range(2):
        extra = jnp.where(c == 0, gram[8 * h : 8 * h + 8], gram[16 + 8 * h : 24 + 8 * h])
        if h == 1:
            extra = jnp.where(row8 == SQ_ROW, sq, extra)
        extra = jnp.where(row8 == FLAG_ROW, mark, extra)
        for j in range(tiles):
            lanes = slice(128 * j, 128 * j + 128)
            ebuf[h * tiles + j, :half] = moment[half * h : half * h + half, lanes]
            ebuf[h * tiles + j, half:] = extra[:, lanes]

    pl.semaphore_wait(barrier, nz + greeted)

    def to_chunk(d):
        p = along(d)
        return pltpu.make_async_remote_copy(
            src_ref=ebuf.at[p], dst_ref=zin.at[z], send_sem=a_send.at[d], recv_sem=a_recv.at[d],
            device_id=(y, x, p, c), device_id_type=MESH,
        )

    for d in far_first:
        to_chunk(d).start()
    for p, low, late in zip(others, lower, later):

        @pl.when((low == 1) & (late == 0))
        def _():
            pl.semaphore_signal(may_send, inc=1, device_id=at_line(p), device_id_type=MESH)

    zin[z] = ebuf[z]

    opened = []
    for r in range(4):
        moment, gram, sq = sums(r)
        square_row = jnp.where(row8 == SQ_ROW, sq, 0.0)
        opened.append(jnp.where(seg_at[r : r + 1] < 0.5, 1.0, 0.0))
        for j in range(tiles):
            lanes = slice(128 * j, 128 * j + 128)
            zsum[r * tiles + j, :n] = moment[:, lanes]
            zsum[r * tiles + j, n : n + 8] = square_row[:, lanes]
            zsum[r * tiles + j, n + 8 :] = gram[:, lanes]
    swap = pltpu.make_async_remote_copy(
        src_ref=zsum.at[:, pl.ds(0, n + 8)], dst_ref=theirs, send_sem=r_send, recv_sem=r_recv,
        device_id=(y, x, z, 1 - c), device_id_type=MESH,
    )
    swap.start()

    flag = half + FLAG_ROW

    def join(earlier, later):
        return earlier * (1.0 - later[flag : flag + 1]) + later

    acc = jnp.zeros((half + 8, 128), jnp.float32)
    for k in range(nz):

        @pl.when(k != z)
        def _():
            to_chunk(lax.rem(z - k + nz, nz)).wait_recv()

        before[k] = acc
        acc = join(acc, zin[k])
    tot[...] = acc

    def to_line(d):
        return pltpu.make_async_remote_copy(
            src_ref=tot, dst_ref=lines.at[line], send_sem=b_send.at[d], recv_sem=b_recv.at[d],
            device_id=at_line(line + d), device_id_type=MESH,
        )


    @pl.when(answers > 0)
    def _():
        pl.semaphore_wait(may_send, answers)

    for p in sorted(range(1, nl), key=lambda p: (p % nx, -p)):

        @pl.when(p > line)
        def _():
            to_line(p - line).start()

    def fold(k, acc):
        to_line(line - k).wait_recv()
        return join(acc, lines[k])

    acc = lax.fori_loop(0, line, fold, jnp.zeros_like(acc))
    for k in range(nz):
        before[k] = join(acc, before[k])
    back[c, z] = before[z]

    def to_date(p, core, send, recv):
        d = lax.rem(p - z + nz, nz)
        return pltpu.make_async_remote_copy(
            src_ref=before.at[p], dst_ref=back.at[c, z], send_sem=send.at[d], recv_sem=recv.at[d],
            device_id=(y, x, p, core), device_id_type=MESH,
        )

    for p in C_ORDER:

        @pl.when(p != z)
        def _():
            to_date(p, c, c_send, c_recv).start()

        to_date(p, 1 - c, x_send, x_recv).start()

    for d in range(1, nl):

        @pl.when(line + d < nl)
        def _():
            to_line(d).wait_send()

    for d in range(1, nz):
        to_chunk(d).wait_send()
        to_date(along(d), c, c_send, c_recv).wait_send()
    for p in range(nz):
        to_date(p, 1 - c, x_send, x_recv).wait_send()

    swap.wait()
    for j in reversed(range(tiles)):
        lanes = slice(128 * j, 128 * j + 128)
        for q in (j, tiles + j):
            p = along(lax.rem(z - q + nz, nz))

            @pl.when(q != z)
            def _():
                to_date(p, c, c_send, c_recv).wait_recv()

            to_date(p, 1 - c, x_send, x_recv).wait_recv()

        by_core = [[back[core, h * tiles + j] for h in range(2)] for core in range(2)]
        pieces = []
        for me in (0, 1):
            moved = [jnp.where(c == me, by_core[0][h], by_core[1][h]) for h in range(2)]
            pieces.append(
                jnp.concatenate([moved[0][:half], moved[1][:half], moved[1][half:]], axis=0)
            )
        pieces.insert(1, jnp.concatenate([t[half:] for t in by_core[0] + by_core[1]], axis=0))
        for r in range(4):
            k = r * tiles + j
            share = opened[r][:, lanes]
            at = k * (48 + 2 * n)
            at_refit[at : at + n + 8] = zsum[k, : n + 8] + share * pieces[0]
            at_refit[at + n + 8 : at + n + 40] = zsum[k, n + 8 :] + share * pieces[1]
            at_refit[at + n + 40 : at + 2 * n + 48] = theirs[k] + share * pieces[2]


def refit_kernel(sizes, at_refit, coef_out, spread_out, coef_v, spread_v, out_sem):
    nb, tiles = sizes
    rows = 8
    each = rows // tiles
    span = nb * tiles * 8
    copies = []
    for part in range(4 // each):
        refit_part(sizes, at_refit, coef_v, spread_v, part * rows, rows)
        there = pl.ds(part * each * span, each * span)
        copy = pltpu.make_async_copy(coef_v.at[there], coef_out.at[there], out_sem.at[part])
        copy.start()
        copies.append(copy)
    copy = pltpu.make_async_copy(spread_v, spread_out, out_sem.at[4 // each])
    copy.start()
    for copy in [*copies, copy]:
        copy.wait()


def refit_part(sizes, at_refit, coef_v, spread_v, first, rows):
    nb, tiles = sizes
    n = 8 * nb
    each = rows // tiles
    stride = 48 + 2 * n

    def load(row):
        return at_refit[pl.ds(first * stride + row, rows, stride=stride), :]

    def got(power, harmonic, shift):
        return load(n + 8 + ROW_OF[(power, harmonic, shift)])

    cosine = [got(0, k, 0) for k in range(7)]
    sine = [None] + [got(0, k, 1) for k in range(1, 7)]
    entry = [[None] * 8 for _ in range(8)]
    entry[0][0] = cosine[0]
    entry[1][0] = got(1, 0, 0)
    entry[1][1] = got(2, 0, 0)
    for k in range(1, 4):
        entry[2 * k][0] = cosine[k]
        entry[2 * k + 1][0] = sine[k]
        entry[2 * k][1] = got(1, k, 0)
        entry[2 * k + 1][1] = got(1, k, 1)
        for m in range(1, k + 1):
            entry[2 * k][2 * m] = 0.5 * (cosine[k - m] + cosine[k + m])
            entry[2 * k + 1][2 * m + 1] = 0.5 * (cosine[k - m] - cosine[k + m])
            if k == m:
                entry[2 * k + 1][2 * m] = 0.5 * sine[2 * k]
            else:
                entry[2 * k + 1][2 * m] = 0.5 * (sine[k + m] + sine[k - m])
                entry[2 * k][2 * m + 1] = 0.5 * (sine[k + m] - sine[k - m])
    inverse = [None] * 8
    for j in range(8):
        diag = entry[j][j] + 1.0 if j == 0 else entry[j][j]
        root = lax.rsqrt(diag)
        root = root * (1.5 - 0.5 * diag * root * root)
        inverse[j] = root
        for i in range(j + 1, 8):
            entry[i][j] = entry[i][j] * root
        for i in range(j + 1, 8):
            for k in range(j + 1, i + 1):
                value = entry[i][k]
                if j == 0 and i == k:
                    value = value + 1.0
                entry[i][k] = value - entry[i][j] * entry[k][j]
    resid = []
    for mine, at in ((True, 0), (False, n + 40)):
        total = load(at + n + SQ_ROW)
        for b in range(nb):
            rhs = [load(at + 8 * b + i) for i in range(8)]
            work = list(rhs)
            for i in range(8):
                work[i] = work[i] * inverse[i]
                for k in range(i + 1, 8):
                    work[k] = work[k] - entry[k][i] * work[i]
            for i in reversed(range(8)):
                work[i] = work[i] * inverse[i]
                for k in range(i):
                    work[k] = work[k] - entry[i][k] * work[i]
            terms = [work[i] * (rhs[i] + work[i]) for i in range(8)]
            while len(terms) > 1:
                terms = [p + q for p, q in zip(terms[::2], terms[1::2])]
            total = total - terms[0]
            if mine:
                for i in range(8):
                    for r in range(each):
                        at_coef = ((first // tiles + r) * nb + b) * tiles * 8 + i
                        piece = work[i][r * tiles : (r + 1) * tiles]
                        coef_v[pl.ds(at_coef, tiles, stride=8), :] = piece
        resid.append(total)
    spread = (resid[0] + resid[1]) / jnp.maximum(cosine[0], 1.0)
    for r in range(each):
        piece = spread[r * tiles : (r + 1) * tiles]
        spread_v[pl.ds(first // tiles + r, tiles, stride=4), :] = piece


def per_device(sizes, observations, valid, breaks, refit):
    dates, nb, px = observations.shape
    ny, nx, nz = sizes
    tiles = px // 128
    assert nz == 2 * tiles
    f32, bf16 = jnp.float32, jnp.bfloat16
    chunk = 4 * nb + 8
    sem = pltpu.SemaphoreType.DMA
    args = (observations, valid, breaks, refit)
    at_refit = pl.pallas_call(
        functools.partial(sum_kernel, sizes, dates * ny * nx * nz),
        out_shape=pltpu.VMEM((4 * tiles * (48 + 16 * nb), 128), f32),
        in_specs=[pl.BlockSpec(memory_space=pltpu.HBM)] * 4,
        out_specs=pl.BlockSpec(memory_space=pltpu.VMEM),
        scratch_shapes=[
            pltpu.VMEM((1, 4), jnp.int32),
            pltpu.VMEM((nb * dates, px), f32),
            pltpu.VMEM((dates, px), jnp.int32),
            pltpu.VMEM((dates, px), jnp.int32),
            pltpu.VMEM((nb * dates, px), bf16),
            pltpu.VMEM((nb * dates, px), bf16),
            pltpu.VMEM((nb * dates, px), bf16),
            pltpu.VMEM((4 * tiles, 40 + 8 * nb, 128), f32),
            pltpu.VMEM((4 * tiles, 8 + 8 * nb, 128), f32),
            pltpu.VMEM((nz, chunk, 128), f32),
            pltpu.VMEM((nz, chunk, 128), f32),
            pltpu.VMEM((nz, chunk, 128), f32),
            pltpu.VMEM((chunk, 128), f32),
            pltpu.VMEM((ny * nx, chunk, 128), f32),
            pltpu.VMEM((2, nz, chunk, 128), f32),
            sem((3 + nb,)),
            sem((nz,)), sem((nz,)),
            sem((ny * nx,)), sem((ny * nx,)),
            sem((nz,)), sem((nz,)),
            sem((nz,)), sem((nz,)),
            sem, sem,
            pltpu.SemaphoreType.REGULAR,
        ],
        compiler_params=pltpu.CompilerParams(
            collective_id=0, has_side_effects=True, vmem_limit_bytes=24 * 1024 * 1024
        ),
    )(*(pltpu.with_memory_space_constraint(a, pltpu.HBM) for a in args))
    coefs, spread = pl.pallas_call(
        functools.partial(refit_kernel, (nb, tiles)),
        out_shape=(pltpu.HBM((32 * nb * tiles, 128), f32), pltpu.HBM((4 * tiles, 128), f32)),
        in_specs=[pl.BlockSpec(memory_space=pltpu.VMEM)],
        out_specs=(pl.BlockSpec(memory_space=pltpu.HBM), pl.BlockSpec(memory_space=pltpu.HBM)),
        scratch_shapes=[
            pltpu.VMEM((32 * nb * tiles, 128), f32),
            pltpu.VMEM((4 * tiles, 128), f32),
            sem((3,)),
        ],
        compiler_params=pltpu.CompilerParams(vmem_limit_bytes=24 * 1024 * 1024),
    )(pltpu.with_memory_space_constraint(at_refit, pltpu.VMEM))
    coefs = jnp.transpose(coefs.reshape(4, nb, tiles, 8, 128), (0, 1, 3, 2, 4))
    spread = jnp.transpose(spread.reshape(tiles, 4, 128), (1, 0, 2))
    return coefs.reshape(1, 4, nb, 8, px), spread.reshape(1, 4, px)


def solution(mesh):
    sizes = (4, 4, 8)
    split = Mesh(mesh.devices.reshape(*sizes, mesh.shape["band"]), (*DATE, "band"))
    placed = (P(DATE, "band", None), P(DATE, None), P(DATE, None), P(DATE, None))
    return jax.shard_map(
        functools.partial(per_device, sizes),
        mesh=split,
        in_specs=placed,
        out_specs=(P(DATE, None, "band", None, None), P(DATE, None, None)),
        check_vma=False,
    )
```

```python
import functools
import math

import jax
import jax.numpy as jnp
from jax import lax
from jax.experimental import pallas as pl
from jax.experimental.pallas import tpu as pltpu
from jax.sharding import Mesh
from jax.sharding import PartitionSpec as P

DATE = ("date_0", "date_1", "date_2")
MESH = pl.DeviceIdType.MESH

GROUPS = (
    ((0, 0, 0), (1, 0, 0), (2, 0, 0), (0, 1, 0), (0, 2, 0), (0, 3, 0)),
    ((0, 1, 1), (0, 2, 1), (0, 3, 1), (0, 4, 0), (0, 5, 0), (0, 6, 0)),
    ((0, 4, 1), (0, 5, 1), (0, 6, 1), (1, 1, 0), (1, 2, 0), (1, 3, 0)),
    ((1, 1, 1), (1, 2, 1), (1, 3, 1)),
)
ROW_OF = {term: 8 * g + k for g, group in enumerate(GROUPS) for k, term in enumerate(group)}
DESIGN = ((0, 0, 0), (1, 0, 0), (0, 1, 0), (0, 1, 1), (0, 2, 0), (0, 2, 1), (0, 3, 0), (0, 3, 1))
SQ_ROW, FLAG_ROW = 6, 7
C_ORDER = (0, 1, 2, 3, 7, 6, 5, 4)


def split3(value):
    high = value.astype(jnp.bfloat16)
    rest = value - high.astype(jnp.float32)
    mid = rest.astype(jnp.bfloat16)
    low = (rest - mid.astype(jnp.float32)).astype(jnp.bfloat16)
    return high, mid, low


def table(terms, rows, first, dates, total):
    row = lax.broadcasted_iota(jnp.int32, (rows, 128), 0)
    lane = lax.broadcasted_iota(jnp.int32, (rows, 128), 1)
    t = (lax.rem(lane, dates) + first).astype(jnp.float32)
    power, harmonic, shift, there = (jnp.zeros((rows, 128), jnp.float32) for _ in range(4))
    for k, term in terms.items():
        here = row == k
        power = jnp.where(here, float(term[0]), power)
        harmonic = jnp.where(here, float(term[1]), harmonic)
        shift = jnp.where(here, float(term[2]), shift)
        there = jnp.where(here, 1.0, there)
    turn = 16.0 * harmonic * t - 1461.0 * shift
    turn = turn - 5844.0 * jnp.floor(turn * (1.0 / 5844.0) + 0.5)
    wave = jnp.cos(turn * (2.0 * math.pi / 5844.0))
    s = 2.0 * (t + 0.5) / total - 1.0
    scale = jnp.where(power > 0.5, s, 1.0) * jnp.where(power > 1.5, s, 1.0)
    return wave * scale * there


def sum_kernel(
    sizes, total,
    obs, valid, breaks, refit, at_refit,
    picked, ov, vv, kv, hi_v, mid_v, lo_v, zsum, theirs, ebuf, zin, before, tot, lines, back,
    in_sem, a_send, a_recv, b_send, b_recv, c_send, c_recv, x_send, x_recv, r_send, r_recv, may_send,
):
    ny, nx, nz = sizes
    nl = ny * nx
    nb, dates, px = ov.shape[0] // vv.shape[0], vv.shape[0], vv.shape[1]
    tiles = px // 128
    y, x, z = (lax.axis_index(a) for a in DATE)
    c = lax.axis_index("band")
    line = y * nx + x
    window = line * nz + z

    def along(d):
        return lax.rem(z + d, nz)

    def at_line(p):
        return (p // nx, lax.rem(p, nx), z, c)

    far_first = sorted(range(1, nz), key=lambda d: -min(d, nz - d))

    barrier = pltpu.get_barrier_semaphore()
    for d in far_first:
        pl.semaphore_signal(barrier, inc=1, device_id=(y, x, along(d), c), device_id_type=MESH)
    pl.semaphore_signal(barrier, inc=1, device_id=(y, x, z, 1 - c), device_id_type=MESH)

    loads = [
        pltpu.make_async_copy(breaks, kv, in_sem.at[0]),
        pltpu.make_async_copy(valid, vv, in_sem.at[1]),
    ]
    for b in range(nb):
        loads.append(
            pltpu.make_async_copy(
                obs.at[:, b, :], ov.at[pl.ds(b * dates, dates), :], in_sem.at[2 + b]
            )
        )
    pick_load = pltpu.make_async_copy(refit, picked, in_sem.at[2 + nb])
    pick_load.start()
    for load in loads:
        load.start()
    def rank(p):
        across, down = lax.rem(p, nx), p // nx
        across = jnp.minimum(across, nx - across)
        return (2 * across + jnp.minimum(down, ny - down)) * nl + p

    mine = rank(line)
    others = [lax.rem(line + d, nl) for d in range(1, nl)]
    lower = [(rank(p) < mine).astype(jnp.int32) for p in others]
    later = [(p > line).astype(jnp.int32) for p in others]
    greeted = sum(lower)
    answers = sum((1 - low) * late for low, late in zip(lower, later))

    for p, low in zip(others, lower):

        @pl.when(low == 0)
        def _():
            pl.semaphore_signal(barrier, inc=1, device_id=at_line(p), device_id_type=MESH)

    first = window * dates
    basis = table({v: k for k, v in ROW_OF.items()}, 32, first, dates, float(total))
    design = table(dict(enumerate(DESIGN)), 8, first, dates, float(total))
    wide = jnp.concatenate([design] * (nb * dates // 128), axis=1)
    wide = jnp.concatenate([wide] * nb, axis=0)
    row = lax.broadcasted_iota(jnp.int32, wide.shape, 0)
    col = lax.broadcasted_iota(jnp.int32, wide.shape, 1)
    wide = jnp.where(row // 8 == col // dates, wide, 0.0)
    wide = jnp.concatenate(split3(wide), axis=0)
    basis = jnp.concatenate(split3(basis[:, :dates]), axis=0)

    pick_load.wait()
    picks = [picked[:, r : r + 1] for r in range(4)]
    reach = lax.broadcasted_iota(jnp.int32, (8 + dates, dates), 0)
    tcol = lax.broadcasted_iota(jnp.int32, (8 + dates, dates), 1)
    upto = reach
    for r in range(4):
        upto = jnp.where(reach == dates + r, picks[r], upto)
    upto = jnp.where(tcol <= upto, 1.0, 0.0).astype(jnp.bfloat16)

    loads[0].wait()
    marks = jnp.dot(
        upto, kv[...].astype(jnp.float32).astype(jnp.bfloat16), preferred_element_type=jnp.float32
    )
    seg = marks[:dates]
    seg_at = marks[dates:]
    loads[1].wait()
    clear = vv[...].astype(jnp.float32)
    for load in loads[2:]:
        load.wait()
    series = ov[...]
    high, mid, low = split3(series)
    hi_v[...] = high
    mid_v[...] = mid
    lo_v[...] = low
    square = series * series
    square = functools.reduce(
        jnp.add, [square[b * dates : (b + 1) * dates] for b in range(nb)]
    )
    trow = lax.broadcasted_iota(jnp.int32, (dates, px), 0)
    n = 8 * nb

    def sums(r):
        inside = seg == seg_at[r : r + 1]
        if r < 4:
            inside = inside & (trow <= picks[r])
        weight = jnp.where(inside, clear, 0.0)
        narrow = weight.astype(jnp.bfloat16)
        tall = jnp.concatenate([narrow] * nb, axis=0)
        one = jnp.dot(wide, tall * hi_v[...], preferred_element_type=jnp.float32)
        two = jnp.dot(wide[: 2 * n], tall * mid_v[...], preferred_element_type=jnp.float32)
        three = jnp.dot(wide[:n], tall * lo_v[...], preferred_element_type=jnp.float32)
        moment = (one[2 * n :] + two[n:] + three) + (one[n : 2 * n] + two[:n]) + one[:n]
        gram = jnp.dot(basis, narrow, preferred_element_type=jnp.float32)
        gram = (gram[64:] + gram[32:64]) + gram[:32]
        sq = jnp.sum(weight * square, axis=0, keepdims=True)
        return moment, gram, sq

    moment, gram, sq = sums(4)
    mark = jnp.where(seg_at[4:5] > 0.5, 1.0, 0.0)
    row8 = lax.broadcasted_iota(jnp.int32, (8, px), 0)
    half = n // 2
    for h in range(2):
        extra = jnp.where(c == 0, gram[8 * h : 8 * h + 8], gram[16 + 8 * h : 24 + 8 * h])
        if h == 1:
            extra = jnp.where(row8 == SQ_ROW, sq, extra)
        extra = jnp.where(row8 == FLAG_ROW, mark, extra)
        for j in range(tiles):
            lanes = slice(128 * j, 128 * j + 128)
            ebuf[h * tiles + j, :half] = moment[half * h : half * h + half, lanes]
            ebuf[h * tiles + j, half:] = extra[:, lanes]

    pl.semaphore_wait(barrier, nz + greeted)

    def to_chunk(d):
        p = along(d)
        return pltpu.make_async_remote_copy(
            src_ref=ebuf.at[p], dst_ref=zin.at[z], send_sem=a_send.at[d], recv_sem=a_recv.at[d],
            device_id=(y, x, p, c), device_id_type=MESH,
        )

    for d in far_first:
        to_chunk(d).start()
    for p, low, late in zip(others, lower, later):

        @pl.when((low == 1) & (late == 0))
        def _():
            pl.semaphore_signal(may_send, inc=1, device_id=at_line(p), device_id_type=MESH)

    zin[z] = ebuf[z]

    opened = []
    for r in range(4):
        moment, gram, sq = sums(r)
        square_row = jnp.where(row8 == SQ_ROW, sq, 0.0)
        opened.append(jnp.where(seg_at[r : r + 1] < 0.5, 1.0, 0.0))
        for j in range(tiles):
            lanes = slice(128 * j, 128 * j + 128)
            zsum[r * tiles + j, :n] = moment[:, lanes]
            zsum[r * tiles + j, n : n + 8] = square_row[:, lanes]
            zsum[r * tiles + j, n + 8 :] = gram[:, lanes]
    swap = pltpu.make_async_remote_copy(
        src_ref=zsum.at[:, pl.ds(0, n + 8)], dst_ref=theirs, send_sem=r_send, recv_sem=r_recv,
        device_id=(y, x, z, 1 - c), device_id_type=MESH,
    )
    swap.start()

    flag = half + FLAG_ROW

    def join(earlier, later):
        return earlier * (1.0 - later[flag : flag + 1]) + later

    acc = jnp.zeros((half + 8, 128), jnp.float32)
    for k in range(nz):

        @pl.when(k != z)
        def _():
            to_chunk(lax.rem(z - k + nz, nz)).wait_recv()

        before[k] = acc
        acc = join(acc, zin[k])
    tot[...] = acc

    def to_line(d):
        return pltpu.make_async_remote_copy(
            src_ref=tot, dst_ref=lines.at[line], send_sem=b_send.at[d], recv_sem=b_recv.at[d],
            device_id=at_line(line + d), device_id_type=MESH,
        )


    @pl.when(answers > 0)
    def _():
        pl.semaphore_wait(may_send, answers)

    for p in sorted(range(1, nl), key=lambda p: (p % nx, -p)):

        @pl.when(p > line)
        def _():
            to_line(p - line).start()

    def fold(k, acc):
        to_line(line - k).wait_recv()
        return join(acc, lines[k])

    acc = lax.fori_loop(0, line, fold, jnp.zeros_like(acc))
    for k in range(nz):
        before[k] = join(acc, before[k])
    back[c, z] = before[z]

    def to_date(p, core, send, recv):
        d = lax.rem(p - z + nz, nz)
        return pltpu.make_async_remote_copy(
            src_ref=before.at[p], dst_ref=back.at[c, z], send_sem=send.at[d], recv_sem=recv.at[d],
            device_id=(y, x, p, core), device_id_type=MESH,
        )

    for p in C_ORDER:

        @pl.when(p != z)
        def _():
            to_date(p, c, c_send, c_recv).start()

        to_date(p, 1 - c, x_send, x_recv).start()

    for d in range(1, nl):

        @pl.when(line + d < nl)
        def _():
            to_line(d).wait_send()

    for d in range(1, nz):
        to_chunk(d).wait_send()
        to_date(along(d), c, c_send, c_recv).wait_send()
    for p in range(nz):
        to_date(p, 1 - c, x_send, x_recv).wait_send()

    swap.wait()
    for j in reversed(range(tiles)):
        lanes = slice(128 * j, 128 * j + 128)
        for q in (j, tiles + j):
            p = along(lax.rem(z - q + nz, nz))

            @pl.when(q != z)
            def _():
                to_date(p, c, c_send, c_recv).wait_recv()

            to_date(p, 1 - c, x_send, x_recv).wait_recv()

        by_core = [[back[core, h * tiles + j] for h in range(2)] for core in range(2)]
        pieces = []
        for me in (0, 1):
            moved = [jnp.where(c == me, by_core[0][h], by_core[1][h]) for h in range(2)]
            pieces.append(
                jnp.concatenate([moved[0][:half], moved[1][:half], moved[1][half:]], axis=0)
            )
        pieces.insert(1, jnp.concatenate([t[half:] for t in by_core[0] + by_core[1]], axis=0))
        for r in range(4):
            k = r * tiles + j
            share = opened[r][:, lanes]
            at = k * (48 + 2 * n)
            at_refit[at : at + n + 8] = zsum[k, : n + 8] + share * pieces[0]
            at_refit[at + n + 8 : at + n + 40] = zsum[k, n + 8 :] + share * pieces[1]
            at_refit[at + n + 40 : at + 2 * n + 48] = theirs[k] + share * pieces[2]


def refit_kernel(sizes, at_refit, coef_out, spread_out, coef_v, spread_v, out_sem):
    nb, tiles = sizes
    rows = 8
    each = rows // tiles
    span = nb * tiles * 8
    copies = []
    for part in range(4 // each):
        there = pl.ds(part * each * span, each * span)
        copy = pltpu.make_async_copy(coef_v.at[there], coef_out.at[there], out_sem.at[part])
        refit_part(sizes, at_refit, coef_v, spread_v, part * rows, rows, copy)
        copies.append(copy)
    copy = pltpu.make_async_copy(spread_v, spread_out, out_sem.at[4 // each])
    copy.start()
    for copy in [*copies, copy]:
        copy.wait()


def refit_part(sizes, at_refit, coef_v, spread_v, first, rows, copy):
    nb, tiles = sizes
    n = 8 * nb
    each = rows // tiles
    stride = 48 + 2 * n

    def load(row):
        return at_refit[pl.ds(first * stride + row, rows, stride=stride), :]

    def got(power, harmonic, shift):
        return load(n + 8 + ROW_OF[(power, harmonic, shift)])

    cosine = [got(0, k, 0) for k in range(7)]
    sine = [None] + [got(0, k, 1) for k in range(1, 7)]
    entry = [[None] * 8 for _ in range(8)]
    entry[0][0] = cosine[0]
    entry[1][0] = got(1, 0, 0)
    entry[1][1] = got(2, 0, 0)
    for k in range(1, 4):
        entry[2 * k][0] = cosine[k]
        entry[2 * k + 1][0] = sine[k]
        entry[2 * k][1] = got(1, k, 0)
        entry[2 * k + 1][1] = got(1, k, 1)
        for m in range(1, k + 1):
            entry[2 * k][2 * m] = 0.5 * (cosine[k - m] + cosine[k + m])
            entry[2 * k + 1][2 * m + 1] = 0.5 * (cosine[k - m] - cosine[k + m])
            if k == m:
                entry[2 * k + 1][2 * m] = 0.5 * sine[2 * k]
            else:
                entry[2 * k + 1][2 * m] = 0.5 * (sine[k + m] + sine[k - m])
                entry[2 * k][2 * m + 1] = 0.5 * (sine[k + m] - sine[k - m])
    inverse = [None] * 8
    for j in range(8):
        diag = entry[j][j] + 1.0 if j == 0 else entry[j][j]
        root = lax.rsqrt(diag)
        root = root * (1.5 - 0.5 * diag * root * root)
        inverse[j] = root
        for i in range(j + 1, 8):
            entry[i][j] = entry[i][j] * root
        for i in range(j + 1, 8):
            for k in range(j + 1, i + 1):
                value = entry[i][k]
                if j == 0 and i == k:
                    value = value + 1.0
                entry[i][k] = value - entry[i][j] * entry[k][j]
    resid = []
    for mine, at in ((True, 0), (False, n + 40)):
        total = load(at + n + SQ_ROW)
        for b in range(nb):
            rhs = [load(at + 8 * b + i) for i in range(8)]
            work = list(rhs)
            for i in range(8):
                work[i] = work[i] * inverse[i]
                for k in range(i + 1, 8):
                    work[k] = work[k] - entry[k][i] * work[i]
            for i in reversed(range(8)):
                work[i] = work[i] * inverse[i]
                for k in range(i):
                    work[k] = work[k] - entry[i][k] * work[i]
            terms = [work[i] * (rhs[i] + work[i]) for i in range(8)]
            while len(terms) > 1:
                terms = [p + q for p, q in zip(terms[::2], terms[1::2])]
            total = total - terms[0]
            if mine:
                for i in range(8):
                    for r in range(each):
                        at_coef = ((first // tiles + r) * nb + b) * tiles * 8 + i
                        piece = work[i][r * tiles : (r + 1) * tiles]
                        coef_v[pl.ds(at_coef, tiles, stride=8), :] = piece
        resid.append(total)
        if mine:
            copy.start()
    spread = (resid[0] + resid[1]) / jnp.maximum(cosine[0], 1.0)
    for r in range(each):
        piece = spread[r * tiles : (r + 1) * tiles]
        spread_v[pl.ds(first // tiles + r, tiles, stride=4), :] = piece


def per_device(sizes, observations, valid, breaks, refit):
    dates, nb, px = observations.shape
    ny, nx, nz = sizes
    tiles = px // 128
    assert nz == 2 * tiles
    f32, bf16 = jnp.float32, jnp.bfloat16
    chunk = 4 * nb + 8
    sem = pltpu.SemaphoreType.DMA
    args = (observations, valid, breaks, refit)
    at_refit = pl.pallas_call(
        functools.partial(sum_kernel, sizes, dates * ny * nx * nz),
        out_shape=pltpu.VMEM((4 * tiles * (48 + 16 * nb), 128), f32),
        in_specs=[pl.BlockSpec(memory_space=pltpu.HBM)] * 4,
        out_specs=pl.BlockSpec(memory_space=pltpu.VMEM),
        scratch_shapes=[
            pltpu.VMEM((1, 4), jnp.int32),
            pltpu.VMEM((nb * dates, px), f32),
            pltpu.VMEM((dates, px), jnp.int32),
            pltpu.VMEM((dates, px), jnp.int32),
            pltpu.VMEM((nb * dates, px), bf16),
            pltpu.VMEM((nb * dates, px), bf16),
            pltpu.VMEM((nb * dates, px), bf16),
            pltpu.VMEM((4 * tiles, 40 + 8 * nb, 128), f32),
            pltpu.VMEM((4 * tiles, 8 + 8 * nb, 128), f32),
            pltpu.VMEM((nz, chunk, 128), f32),
            pltpu.VMEM((nz, chunk, 128), f32),
            pltpu.VMEM((nz, chunk, 128), f32),
            pltpu.VMEM((chunk, 128), f32),
            pltpu.VMEM((ny * nx, chunk, 128), f32),
            pltpu.VMEM((2, nz, chunk, 128), f32),
            sem((3 + nb,)),
            sem((nz,)), sem((nz,)),
            sem((ny * nx,)), sem((ny * nx,)),
            sem((nz,)), sem((nz,)),
            sem((nz,)), sem((nz,)),
            sem, sem,
            pltpu.SemaphoreType.REGULAR,
        ],
        compiler_params=pltpu.CompilerParams(
            collective_id=0, has_side_effects=True, vmem_limit_bytes=24 * 1024 * 1024
        ),
    )(*(pltpu.with_memory_space_constraint(a, pltpu.HBM) for a in args))
    coefs, spread = pl.pallas_call(
        functools.partial(refit_kernel, (nb, tiles)),
        out_shape=(pltpu.HBM((32 * nb * tiles, 128), f32), pltpu.HBM((4 * tiles, 128), f32)),
        in_specs=[pl.BlockSpec(memory_space=pltpu.VMEM)],
        out_specs=(pl.BlockSpec(memory_space=pltpu.HBM), pl.BlockSpec(memory_space=pltpu.HBM)),
        scratch_shapes=[
            pltpu.VMEM((32 * nb * tiles, 128), f32),
            pltpu.VMEM((4 * tiles, 128), f32),
            sem((3,)),
        ],
        compiler_params=pltpu.CompilerParams(vmem_limit_bytes=24 * 1024 * 1024),
    )(pltpu.with_memory_space_constraint(at_refit, pltpu.VMEM))
    coefs = jnp.transpose(coefs.reshape(4, nb, tiles, 8, 128), (0, 1, 3, 2, 4))
    spread = jnp.transpose(spread.reshape(tiles, 4, 128), (1, 0, 2))
    return coefs.reshape(1, 4, nb, 8, px), spread.reshape(1, 4, px)


def solution(mesh):
    sizes = (4, 4, 8)
    split = Mesh(mesh.devices.reshape(*sizes, mesh.shape["band"]), (*DATE, "band"))
    placed = (P(DATE, "band", None), P(DATE, None), P(DATE, None), P(DATE, None))
    return jax.shard_map(
        functools.partial(per_device, sizes),
        mesh=split,
        in_specs=placed,
        out_specs=(P(DATE, None, "band", None, None), P(DATE, None, None)),
        check_vma=False,
    )
```
